256 devices in a mesh: ctx: 16 (over z, y_hi), smp: 16 (over x, y_lo, core).
Axes of the slice: x: 4, y: 4 (y_hi: 2, y_lo: 2; y = y_hi * 2 + y_lo), z: 8, core: 2. Of those that a mesh axis runs over, the one named last changes fastest.
Arguments:
- prompt_inputs: bfloat16 [32768, 4096], P('ctx', 'smp'), may hold values from -0.59765625 to 0.59765625
- prompt_outgrad: bfloat16 [32768, 4096], P('ctx', 'smp'), may hold values from -0.29882812 to 0.29882812
- prompt_bproj: bfloat16 [32768, 128], P('ctx'), may hold values from -0.5 to 0.5
- prompt_cproj: bfloat16 [32768, 128], P('ctx'), may hold values from -0.5 to 0.5
- prompt_decay: float32 [64, 32768], P('smp', 'ctx'), may hold values from -0.7 to 0, as said below
- prompt_states: float32 [16, 64, 8192], P('ctx', 'smp'), may hold values from -3 to 3
- answer_inputs: bfloat16 [16, 2048, 4096], P('smp', None, 'ctx'), may hold values from -0.59765625 to 0.59765625
- answer_outgrad: bfloat16 [16, 2048, 4096], P('smp', None, 'ctx'), may hold values from -0.29882812 to 0.29882812
- answer_bproj: bfloat16 [16, 2048, 128], P('smp'), may hold values from -0.5 to 0.5
- answer_cproj: bfloat16 [16, 2048, 128], P('smp'), may hold values from -0.5 to 0.5
- answer_decay: float32 [16, 64, 2048], P('smp', 'ctx'), may hold values from -0.7 to 0, as said below
- answer_state: float32 [64, 8192], P('ctx'), may hold values from -3 to 3
Outputs:
- prompt_xgrad: float32 [32768, 4096], P('ctx', 'smp')
- prompt_bgrad: float32 [32768, 128], P(('ctx', 'smp'))
- prompt_cgrad: float32 [32768, 128], P(('ctx', 'smp'))
- answer_xgrad: float32 [16, 2048, 4096], P('smp', None, 'ctx')
- answer_bgrad: float32 [16, 2048, 128], P('smp', 'ctx')
- answer_cgrad: float32 [16, 2048, 128], P('smp', 'ctx')
The draws below stay inside these ranges and needn't reach their ends.
Inputs may be any that keep to these rules, and one draw needn't show every extreme that they name: `prompt_decay`: log decay factors; none is positive. `answer_decay`: log decay factors; none is positive.
All inputs are finite; a program needn't handle non-finite values.
Results may differ from the reference program's by a relative error of at most 0.007.
Values sent between devices are 32-bit elements; how exact they have to be, the bound alone decides.
No kernel may reach another device: no remote copies, remote signals or barrier semaphores. Data moves between devices by JAX's collectives and lax.ppermute only.
A program may use at most 128 MiB of HBM per device.

```python
import jax
import jax.numpy as jnp
from jax import lax

HEADS = 64
HEAD_DIM = 64
STATE = 128
BLOCK = 256
TOK_DEV = 2048
ANSWER_LEN = 2048
QUESTION_LENGTH = 32768
ANSWERS = 16
N_CTX = 16


def head_rates(key, fast_share):
    key = jax.random.fold_in(key, 101)
    pick_key, fast_key, slow_key = jax.random.split(key, 3)
    fast = jax.random.bernoulli(pick_key, fast_share, (HEADS,))
    fast_rate = jnp.exp(jax.random.uniform(fast_key, (HEADS,), jnp.float32, jnp.log(1.0 / 50.0), jnp.log(1.0 / 30.0)))
    slow_rate = jax.random.uniform(slow_key, (HEADS,), jnp.float32, 0.03, 0.12) / QUESTION_LENGTH
    return jnp.where(fast, fast_rate, slow_rate)


def decay_logs(key, forgetting_speeds, tensor_dimensions):
    perturbation_seed_handle, spike_seed_handle, strength_seed_handle = jax.random.split(key, 3)
    small_perturbation = jnp.exp(jax.random.uniform(perturbation_seed_handle, tensor_dimensions, jnp.float32, -0.7, 0.7))
    spike_multiplier = jax.random.bernoulli(spike_seed_handle, 2.0 / QUESTION_LENGTH, tensor_dimensions)
    forgetting_strength = jax.random.uniform(strength_seed_handle, tensor_dimensions, jnp.float32, jnp.log(0.55), jnp.log(0.8))
    return -forgetting_speeds * small_perturbation + jnp.where(spike_multiplier, forgetting_strength, 0.0)


def draw_prompt_decay(key, part):
    share = 0.5
    forgetting_speeds = head_rates(key, share)
    key = jax.random.fold_in(key, 3)
    return decay_logs(key, forgetting_speeds[:, None], (HEADS, QUESTION_LENGTH))


def draw_answer_decay(key, part):
    share = 0.5
    forgetting_speeds = head_rates(key, share)
    key = jax.random.fold_in(key, 5)
    return decay_logs(key, forgetting_speeds[None, :, None], (ANSWERS, HEADS, ANSWER_LEN))


def block_scale(rng, dims, cuts, least, largest):
    factor_of, own = 1.0, jax.random.fold_in(rng, 6)
    for axis_at, shards_of in cuts:
        steps = jnp.exp(jax.random.uniform(jax.random.fold_in(own, axis_at), (shards_of,), jnp.float32, least / len(cuts), largest / len(cuts)))
        factor_of = factor_of * jnp.repeat(steps, dims[axis_at] // shards_of).reshape([-1 if axis == axis_at else 1 for axis in range(len(dims))])
    return factor_of


def scatter_about(own_key, shape, width, reach, shards=(), held_as=jnp.bfloat16):
    entries = jax.random.normal(own_key, shape, jnp.float32) * width
    if len(shards) > 0:
        entries = block_scale(own_key, shape, shards, -0.22, 0.18) * entries
    return jnp.clip(entries, min=-reach, max=reach).astype(held_as)


def setup_inputs(seed: int = 0) -> dict:
    key_list = jax.random.split(jax.random.key(seed), 13)
    return {
        "prompt_inputs": scatter_about(key_list[0], (QUESTION_LENGTH, HEADS * HEAD_DIM), 0.1, 0.59765625, ((0, 16), (1, 16))),
        "prompt_outgrad": scatter_about(key_list[1], (QUESTION_LENGTH, HEADS * HEAD_DIM), 0.05, 0.29882812, ((0, 16), (1, 16))),
        "prompt_bproj": scatter_about(key_list[2], (QUESTION_LENGTH, STATE), STATE ** -0.5, 0.5, ((0, 16),)),
        "prompt_cproj": scatter_about(key_list[3], (QUESTION_LENGTH, STATE), STATE ** -0.5, 0.5, ((0, 16),)),
        "prompt_decay": draw_prompt_decay(jax.random.fold_in(key_list[12], 71), 0),
        "prompt_states": scatter_about(key_list[5], (N_CTX, HEADS, STATE * HEAD_DIM), 0.5, 3.0, ((0, 16), (1, 16)), jnp.float32),
        "answer_inputs": scatter_about(key_list[6], (ANSWERS, ANSWER_LEN, HEADS * HEAD_DIM), 0.1, 0.59765625, ((0, 16), (2, 16))),
        "answer_outgrad": scatter_about(key_list[7], (ANSWERS, ANSWER_LEN, HEADS * HEAD_DIM), 0.05, 0.29882812, ((0, 16), (2, 16))),
        "answer_bproj": scatter_about(key_list[8], (ANSWERS, ANSWER_LEN, STATE), STATE ** -0.5, 0.5, ((0, 16),)),
        "answer_cproj": scatter_about(key_list[9], (ANSWERS, ANSWER_LEN, STATE), STATE ** -0.5, 0.5, ((0, 16),)),
        "answer_decay": draw_answer_decay(jax.random.fold_in(key_list[12], 71), 0),
        "answer_state": scatter_about(key_list[11], (HEADS, STATE * HEAD_DIM), 0.5, 3.0, ((0, 16),), jnp.float32),
    }


HIGH = lax.Precision.HIGHEST


def block_state(x_rows, b_rows, logs, state_in):
    running = jnp.cumsum(logs, axis=1)
    final = running[:, -1:]
    to_end = jnp.exp(final - running)
    scaled = to_end[:, :, None] * b_rows.astype(jnp.float32)[None]
    fresh = jnp.einsum('hsn,shp->hnp', scaled, x_rows.astype(jnp.float32), precision=HIGH)
    return jnp.exp(final)[:, :, None] * state_in + fresh


def block_terms(x_rows, dy_rows, b_rows, c_rows, logs, state_in, grad_in):
    span_len = logs.shape[1]
    running = jnp.cumsum(logs, axis=1)
    final = running[:, -1:]
    row_ids = lax.broadcasted_iota(jnp.int32, (span_len, span_len), 0)
    col_ids = lax.broadcasted_iota(jnp.int32, (span_len, span_len), 1)
    causal = col_ids >= row_ids
    weight = jnp.exp(jnp.where(causal[None], running[:, None, :] - running[:, :, None], -jnp.inf))
    inner_bc = jnp.dot(b_rows, c_rows.T, preferred_element_type=jnp.float32)
    x_wide = x_rows.astype(jnp.float32)
    dy_wide = dy_rows.astype(jnp.float32)
    inner_xy = jnp.einsum('thp,shp->hts', x_wide, dy_wide)
    x_coeffs = (weight * inner_bc[None]).astype(jnp.bfloat16)
    weighted = (weight * inner_xy).astype(jnp.bfloat16)
    to_end = jnp.exp(final - running)
    from_start = jnp.exp(running)
    b_wide = b_rows.astype(jnp.float32)
    c_wide = c_rows.astype(jnp.float32)
    grad_x = jnp.einsum('hts,shp->thp', x_coeffs.astype(jnp.float32), dy_wide)
    grad_x = grad_x + to_end.T[:, :, None] * jnp.einsum('tn,hnp->thp', b_wide, grad_in, precision=HIGH)
    grad_b = jnp.einsum('hts,sn->tn', weighted.astype(jnp.float32), c_wide)
    grad_b = grad_b + jnp.einsum('thp,hnp->tn', x_wide * to_end.T[:, :, None], grad_in, precision=HIGH)
    grad_c = jnp.einsum('hst,sn->tn', weighted.astype(jnp.float32), b_wide)
    grad_c = grad_c + jnp.einsum('thp,hnp->tn', dy_wide * from_start.T[:, :, None], state_in, precision=HIGH)
    grad_out = jnp.einsum('hsn,shp->hnp', from_start[:, :, None] * c_wide[None], dy_wide, precision=HIGH)
    grad_out = grad_out + jnp.exp(final)[:, :, None] * grad_in
    return grad_x, grad_b, grad_c, grad_out


def split_rows(inputs, bproj, decay, span_len):
    count = inputs.shape[0] // span_len
    heads = inputs.shape[1]
    x_blocks = inputs.reshape(count, span_len, heads, inputs.shape[2])
    b_blocks = bproj.reshape(count, span_len, bproj.shape[1])
    log_blocks = decay.reshape(heads, count, span_len).transpose(1, 0, 2)
    return x_blocks, b_blocks, log_blocks


def forward_states(inputs, bproj, decay, start, span_len):
    x_blocks, b_blocks, log_blocks = split_rows(inputs, bproj, decay, span_len)

    def advance(state, pieces):
        return block_state(pieces[0], pieces[1], pieces[2], state), state

    _, states = lax.scan(advance, start, (x_blocks, b_blocks, log_blocks))
    return states


def backward(inputs, outgrad, bproj, cproj, decay, states, grad_end, span_len):
    x_blocks, b_blocks, log_blocks = split_rows(inputs, bproj, decay, span_len)
    dy_blocks, c_blocks, _ = split_rows(outgrad, cproj, decay, span_len)

    def advance(carried, pieces):
        grad_x, grad_b, grad_c, fresh = block_terms(pieces[0], pieces[1], pieces[2], pieces[3], pieces[4], pieces[5], carried)
        return fresh, (grad_x, grad_b, grad_c)

    first, (grad_x, grad_b, grad_c) = lax.scan(advance, grad_end, (x_blocks, dy_blocks, b_blocks, c_blocks, log_blocks, states), reverse=True)
    length = inputs.shape[0]
    return grad_x.reshape(length, inputs.shape[1], inputs.shape[2]), grad_b.reshape(length, -1), grad_c.reshape(length, -1), first


def reference(prompt_inputs, prompt_outgrad, prompt_bproj, prompt_cproj, prompt_decay, prompt_states, answer_inputs, answer_outgrad, answer_bproj, answer_cproj, answer_decay, answer_state):
    answer_start = answer_state.reshape(HEADS, STATE, HEAD_DIM)
    zero_grad = jnp.zeros((HEADS, STATE, HEAD_DIM), jnp.float32)

    def one_answer(pieces):
        inputs = pieces[0].reshape(ANSWER_LEN, HEADS, HEAD_DIM)
        outgrad = pieces[1].reshape(ANSWER_LEN, HEADS, HEAD_DIM)
        states = forward_states(inputs, pieces[2], pieces[4], answer_start, BLOCK)
        grad_x, grad_b, grad_c, first = backward(inputs, outgrad, pieces[2], pieces[3], pieces[4], states, zero_grad, BLOCK)
        return grad_x.reshape(ANSWER_LEN, HEADS * HEAD_DIM), grad_b, grad_c, first

    answer_xgrad, answer_bgrad, answer_cgrad, firsts = lax.map(one_answer, (answer_inputs, answer_outgrad, answer_bproj, answer_cproj, answer_decay))
    answer_total = jnp.sum(firsts, axis=0)
    inputs = prompt_inputs.reshape(QUESTION_LENGTH, HEADS, HEAD_DIM)
    outgrad = prompt_outgrad.reshape(QUESTION_LENGTH, HEADS, HEAD_DIM)
    shard_x = inputs.reshape(N_CTX, TOK_DEV, HEADS, HEAD_DIM)
    shard_b = prompt_bproj.reshape(N_CTX, TOK_DEV, STATE)
    shard_logs = prompt_decay.reshape(HEADS, N_CTX, TOK_DEV).transpose(1, 0, 2)
    shard_start = prompt_states.reshape(N_CTX, HEADS, STATE, HEAD_DIM)

    def one_shard(pieces):
        return forward_states(pieces[0], pieces[1], pieces[2], pieces[3], BLOCK)

    states = lax.map(one_shard, (shard_x, shard_b, shard_logs, shard_start))
    states = states.reshape(QUESTION_LENGTH // BLOCK, HEADS, STATE, HEAD_DIM)
    grad_x, grad_b, grad_c, _ = backward(inputs, outgrad, prompt_bproj, prompt_cproj, prompt_decay, states, answer_total, BLOCK)
    return (grad_x.reshape(QUESTION_LENGTH, HEADS * HEAD_DIM), grad_b, grad_c, answer_xgrad, answer_bgrad, answer_cgrad)
```

```python
import jax
import jax.numpy as jnp
from jax import lax
from jax.experimental import pallas as pl
from jax.experimental.pallas import tpu as pltpu
from jax.sharding import Mesh, PartitionSpec as P

CTX = ("z", "yh")
SMP = ("x", "yl", "core")
HEAD_DIM = 64
STATE = 128
BLOCK = 256
HEADS_DEV = 4
WIDTH = HEADS_DEV * HEAD_DIM
LANES = 128
F32 = jnp.float32
BF16 = jnp.bfloat16
VMEM_LIMIT = 40 * 1024 * 1024


def iota(shape, dim):
    return lax.broadcasted_iota(jnp.int32, shape, dim)


def dot(a, b, dims=((1,), (0,))):
    return lax.dot_general(a, b, (dims, ((), ())), preferred_element_type=F32)


def split3(v):
    first = v.astype(BF16)
    rest = v - first.astype(F32)
    second = rest.astype(BF16)
    third = (rest - second.astype(F32)).astype(BF16)
    return first, second, third


def split2(v):
    first = v.astype(BF16)
    return first, (v - first.astype(F32)).astype(BF16)


def running_sums(logs):
    upper = (iota((BLOCK, BLOCK), 0) <= iota((BLOCK, BLOCK), 1)).astype(BF16)
    padded = jnp.concatenate([logs, logs, logs, logs], axis=0)
    one, two, three = split3(padded)
    rows = (dot(one, upper) + dot(two, upper) + dot(three, upper))[0:8]
    cols = rows.T
    spread = [jnp.broadcast_to(cols[:, h : h + 1], (BLOCK, LANES)) for h in range(HEADS_DEV)]
    return rows, spread


def by_channel(spread):
    low = iota((BLOCK, LANES), 1) < HEAD_DIM
    return jnp.concatenate(
        [jnp.where(low, spread[0], spread[1]), jnp.where(low, spread[2], spread[3])], axis=1
    )


def pieces_of(state):
    return [state[:, k * LANES : (k + 1) * LANES].reshape(16, 8, LANES) for k in range(2)]


def carry_kernel(dy_ref, c_ref, logs_ref, r_ref, cum_ref, first_ref, r_scr, d_scr):
    step = pl.program_id(0)

    @pl.when(step == 0)
    def _():
        r_scr[...] = jnp.zeros_like(r_scr)
        d_scr[...] = jnp.ones_like(d_scr)

    _, spread = running_sums(logs_ref[...])
    run = by_channel(spread)
    high, low = split2(dy_ref[...].astype(F32) * jnp.exp(run))
    turned = c_ref[...].T
    final = jnp.exp(run[BLOCK - 1 : BLOCK])
    r_ref[0] = r_scr[...]
    cum_ref[0] = d_scr[...]
    r_scr[...] = final * r_scr[...] + (dot(turned, high) + dot(turned, low))
    d_scr[...] = final * d_scr[...]

    @pl.when(step == pl.num_programs(0) - 1)
    def _():
        state = r_scr[...]
        dec = d_scr[...]
        for k in range(2):
            first_ref[:, k] = state[:, k * LANES : (k + 1) * LANES].reshape(16, 8, LANES)
            first_ref[:, 2 + k] = jnp.broadcast_to(dec[None, :, k * LANES : (k + 1) * LANES], (16, 8, LANES))


def carry(dy, c, logs):
    blocks = dy.shape[0] // BLOCK
    back = lambda i: (blocks - 1 - i, 0)
    return pl.pallas_call(
        carry_kernel,
        grid=(blocks,),
        in_specs=[
            pl.BlockSpec((BLOCK, WIDTH), back),
            pl.BlockSpec((BLOCK, STATE), back),
            pl.BlockSpec((HEADS_DEV, BLOCK), lambda i: (0, blocks - 1 - i)),
        ],
        out_specs=[
            pl.BlockSpec((1, STATE, WIDTH), lambda i: (blocks - 1 - i, 0, 0)),
            pl.BlockSpec((1, 8, WIDTH), lambda i: (blocks - 1 - i, 0, 0)),
            pl.BlockSpec((16, 4, 8, LANES), lambda i: (0, 0, 0, 0)),
        ],
        out_shape=[
            jax.ShapeDtypeStruct((blocks, STATE, WIDTH), F32),
            jax.ShapeDtypeStruct((blocks, 8, WIDTH), F32),
            jax.ShapeDtypeStruct((16, 4, 8, LANES), F32),
        ],
        scratch_shapes=[pltpu.VMEM((STATE, WIDTH), F32), pltpu.VMEM((8, WIDTH), F32)],
        compiler_params=pltpu.CompilerParams(vmem_limit_bytes=VMEM_LIMIT),
    )(dy, c, logs)


def load_state(s0_ref, m_scr):
    for r in range(64):
        m_scr[4 * r : 4 * r + 4] = s0_ref[:, LANES * r : LANES * (r + 1)]
    low = iota((64, LANES), 1) < HEAD_DIM
    halves = []
    for k in range(2):
        one = m_scr[pl.ds(2 * k, 64, stride=4), :]
        two = m_scr[pl.ds(2 * k + 1, 64, stride=4), :]
        even = jnp.where(low, one, pltpu.roll(two, HEAD_DIM, 1))
        odd = jnp.where(low, pltpu.roll(one, HEAD_DIM, 1), two)
        halves.append(jnp.concatenate([even, odd], axis=0))
    parted = jnp.concatenate(halves, axis=1)
    row, col = iota((STATE, STATE), 0), iota((STATE, STATE), 1)
    order = (col == (row & 1) * 64 + (row >> 1)).astype(BF16)
    one, two, three = split3(parted)
    return dot(order, one) + dot(order, two) + dot(order, three)


def main_body(x_ref, dy_ref, b_ref, c_ref, logs_ref, r_in, s0_ref, gx_ref, s_scr, m_scr):
    step = pl.program_id(0)

    @pl.when(step == 0)
    def _():
        s_scr[...] = load_state(s0_ref, m_scr)

    half = BLOCK // 2
    x, dy, b, c = x_ref[...], dy_ref[...], b_ref[...], c_ref[...]
    rows, spread = running_sums(logs_ref[...])
    run = by_channel(spread)
    final = run[BLOCK - 1 : BLOCK]
    to_end = jnp.exp(final - run)
    x_high, x_low = split2(x.astype(F32) * to_end)
    dy_high, dy_low = split2(dy.astype(F32) * jnp.exp(run))
    r_both = jnp.concatenate(split2(r_in), axis=0)
    state = s_scr[...]
    s_both = jnp.concatenate(split2(state), axis=0)
    turned = b.T
    s_scr[...] = jnp.exp(final) * state + (dot(turned, x_high) + dot(turned, x_low))

    bc_top = dot(b[:half], c, ((1,), (1,)))
    bc_bot = dot(b[half:], c[half:], ((1,), (1,)))
    keep_top = iota((half, BLOCK), 1) >= iota((half, BLOCK), 0)
    keep_bot = iota((half, half), 1) >= iota((half, half), 0)
    lane = iota((BLOCK, WIDTH), 1)
    lane_half = iota((BLOCK, LANES), 1)
    coeff_top, coeff_bot, dy_top, dy_bot = [], [], [], []
    sum_top = jnp.zeros((half, BLOCK), F32)
    sum_bot = jnp.zeros((half, half), F32)
    zero = jnp.zeros((), BF16)
    for h in range(HEADS_DEV):
        pair = slice((h // 2) * LANES, (h // 2 + 1) * LANES)
        mine = (lane_half < HEAD_DIM) if h % 2 == 0 else (lane_half >= HEAD_DIM)
        x_h = jnp.where(mine, x[:, pair], zero)
        dy_pair = dy[:, pair]
        dy_h = jnp.where((lane >= h * HEAD_DIM) & (lane < (h + 1) * HEAD_DIM), dy, zero)
        row = rows[h : h + 1]
        col_top = jnp.concatenate([spread[h][:half], spread[h][:half]], axis=1)
        w_top = jnp.where(keep_top, jnp.exp(row - col_top), 0.0)
        w_bot = jnp.where(keep_bot, jnp.exp(row[:, half:] - spread[h][half:]), 0.0)
        xy_top = dot(x_h[:half], dy_pair, ((1,), (1,)))
        xy_bot = dot(x_h[half:], dy_pair[half:], ((1,), (1,)))
        coeff_top.append((w_top * bc_top).astype(BF16))
        coeff_bot.append((w_bot * bc_bot).astype(BF16))
        sum_top = sum_top + w_top * xy_top
        sum_bot = sum_bot + w_bot * xy_bot
        dy_top.append(dy_h)
        dy_bot.append(dy_h[half:])

    from_r = to_end * dot(jnp.concatenate([b, b], axis=1), r_both)
    gx_ref[:half] = from_r[:half] + dot(jnp.concatenate(coeff_top, axis=1), jnp.concatenate(dy_top, axis=0))
    gx_ref[half:] = from_r[half:] + dot(jnp.concatenate(coeff_bot, axis=1), jnp.concatenate(dy_bot, axis=0))
    w_top = sum_top.astype(BF16)
    w_bot = sum_bot.astype(BF16)
    b_state = dot(x_high, r_both, ((1,), (1,)))
    b_state = b_state[:, :STATE] + b_state[:, STATE:] + dot(x_low, r_both[:STATE], ((1,), (1,)))
    c_state = dot(dy_high, s_both, ((1,), (1,)))
    c_state = c_state[:, :STATE] + c_state[:, STATE:] + dot(dy_low, s_both[:STATE], ((1,), (1,)))
    b_top = b_state[:half] + dot(w_top, c)
    b_bot = b_state[half:] + dot(w_bot, c[half:])
    c_top = c_state[:half] + dot(w_top[:, :half], b[:half], ((0,), (0,)))
    c_bot = (
        c_state[half:]
        + dot(w_top[:, half:], b[:half], ((0,), (0,)))
        + dot(w_bot, b[half:], ((0,), (0,)))
    )
    return b_top, b_bot, c_top, c_bot


def answer_kernel(x_ref, dy_ref, b_ref, c_ref, logs_ref, r_ref, s0_ref, gx_ref, bc_ref, s_scr, m_scr):
    b_top, b_bot, c_top, c_bot = main_body(
        x_ref, dy_ref, b_ref, c_ref, logs_ref, r_ref[0], s0_ref, gx_ref, s_scr, m_scr
    )
    bc_ref[0, 0:LANES] = b_top
    bc_ref[0, LANES:] = c_top
    bc_ref[1, 0:LANES] = b_bot
    bc_ref[1, LANES:] = c_bot


def prompt_kernel(
    x_ref, dy_ref, b_ref, c_ref, logs_ref, r_ref, s0_ref, cum_ref, g_ref, core_ref, gx_ref, keep_ref, send_ref, s_scr, m_scr, g_scr
):
    @pl.when(pl.program_id(0) == 0)
    def _():
        for k in range(2):
            g_scr[:, k * LANES : (k + 1) * LANES] = g_ref[:, k].reshape(STATE, LANES)

    r_in = r_ref[0] + cum_ref[0, 0:1] * g_scr[...]
    b_top, b_bot, c_top, c_bot = main_body(
        x_ref, dy_ref, b_ref, c_ref, logs_ref, r_in, s0_ref, gx_ref, s_scr, m_scr
    )
    first = core_ref[0] == 0
    keep_ref[0, 0:LANES] = jnp.where(first, b_top, b_bot)
    keep_ref[0, LANES:] = jnp.where(first, c_top, c_bot)
    send_ref[0, 0:LANES] = jnp.where(first, b_bot, b_top)
    send_ref[0, LANES:] = jnp.where(first, c_bot, c_top)


def main_specs(blocks):
    return [
        pl.BlockSpec((BLOCK, WIDTH), lambda i: (i, 0)),
        pl.BlockSpec((BLOCK, WIDTH), lambda i: (i, 0)),
        pl.BlockSpec((BLOCK, STATE), lambda i: (i, 0)),
        pl.BlockSpec((BLOCK, STATE), lambda i: (i, 0)),
        pl.BlockSpec((HEADS_DEV, BLOCK), lambda i: (0, i)),
        pl.BlockSpec((1, STATE, WIDTH), lambda i: (i, 0, 0)),
        pl.BlockSpec((HEADS_DEV, STATE * HEAD_DIM), lambda i: (0, 0)),
    ]


def main_call(kernel, extra_specs, extra_scratch, sums, args):
    blocks = args[0].shape[0] // BLOCK
    return pl.pallas_call(
        kernel,
        grid=(blocks,),
        in_specs=main_specs(blocks) + extra_specs,
        out_specs=[pl.BlockSpec((BLOCK, WIDTH), lambda i: (i, 0))]
        + [pl.BlockSpec((2 // sums, BLOCK, LANES), lambda i: (i, 0, 0))] * sums,
        out_shape=[jax.ShapeDtypeStruct((blocks * BLOCK, WIDTH), F32)]
        + [jax.ShapeDtypeStruct((2 // sums * blocks, BLOCK, LANES), F32)] * sums,
        scratch_shapes=[pltpu.VMEM((STATE, WIDTH), F32), pltpu.VMEM((256, LANES), F32)] + extra_scratch,
        compiler_params=pltpu.CompilerParams(vmem_limit_bytes=VMEM_LIMIT),
    )(*args)


def answer_call(*args):
    return main_call(answer_kernel, [], [], 1, args)


def prompt_call(*args):
    extra = [
        pl.BlockSpec((1, 8, WIDTH), lambda i: (i, 0, 0)),
        pl.BlockSpec((16, 2, 8, LANES), lambda i: (0, 0, 0, 0)),
        pl.BlockSpec(memory_space=pltpu.SMEM),
    ]
    return main_call(prompt_kernel, extra, [pltpu.VMEM((STATE, WIDTH), F32)], 2, args)


def scan_kernel(in_ref, out_ref):
    for k in range(2):
        grad = in_ref[0, 4 + k]
        for a in range(1, 16):
            grad = grad + in_ref[a, 4 + k]
        for j in range(15, -1, -1):
            out_ref[j, k] = grad
            grad = in_ref[j, k] + in_ref[j, 2 + k] * grad


def scan_call(pieces):
    return pl.pallas_call(
        scan_kernel,
        out_shape=jax.ShapeDtypeStruct((16, 2, 8, LANES), F32),
        compiler_params=pltpu.CompilerParams(vmem_limit_bytes=VMEM_LIMIT),
    )(pieces)


def swap(v, axis):
    return lax.all_to_all(v, axis, 0, 0, tiled=True)


def local(
    prompt_inputs,
    prompt_outgrad,
    prompt_bproj,
    prompt_cproj,
    prompt_decay,
    prompt_states,
    answer_inputs,
    answer_outgrad,
    answer_bproj,
    answer_cproj,
    answer_decay,
    answer_state,
):
    a_r, _, a_first = carry(answer_outgrad[0], answer_cproj[0], answer_decay[0])
    turn = [(c * 16 + s, s * 16 + c) for c in range(16) for s in range(16)]
    a_turned = lax.ppermute(a_first[:, 0:2], CTX + SMP, turn)
    p_r, p_cum, p_first = carry(prompt_outgrad, prompt_cproj, prompt_decay)
    answer_gx, answer_bc = answer_call(
        answer_inputs[0],
        answer_outgrad[0],
        answer_bproj[0],
        answer_cproj[0],
        answer_decay[0],
        a_r,
        answer_state,
    )
    answer_sum = lax.psum_scatter(answer_bc, "z", scatter_dimension=0, tiled=True)
    answer_sum = lax.psum_scatter(answer_sum, "yh", scatter_dimension=0, tiled=True)
    grads = scan_call(swap(jnp.concatenate([p_first, a_turned], axis=1), CTX))
    entering = swap(grads, CTX)
    core = lax.axis_index("core").astype(jnp.int32)[None]
    prompt_gx, keep, send = prompt_call(
        prompt_inputs,
        prompt_outgrad,
        prompt_bproj,
        prompt_cproj,
        prompt_decay,
        p_r,
        prompt_states[0],
        p_cum,
        entering,
        core,
    )
    chip = keep + lax.ppermute(send, "core", [(0, 1), (1, 0)])
    prompt_sum = jnp.sum(swap(chip, ("x", "yl")), axis=0)
    return (
        prompt_gx,
        prompt_sum[:LANES],
        prompt_sum[LANES:],
        answer_gx[None],
        answer_sum[:, :LANES],
        answer_sum[:, LANES:],
    )


def solution(mesh):
    split = Mesh(mesh.devices.reshape(8, 2, 4, 2, 2), CTX + SMP)
    in_specs = (
        P(CTX, SMP),
        P(CTX, SMP),
        P(CTX, None),
        P(CTX, None),
        P(SMP, CTX),
        P(CTX, SMP, None),
        P(SMP, None, CTX),
        P(SMP, None, CTX),
        P(SMP, None, None),
        P(SMP, None, None),
        P(SMP, CTX, None),
        P(CTX, None),
    )
    out_specs = (
        P(CTX, SMP),
        P(CTX + SMP, None),
        P(CTX + SMP, None),
        P(SMP, None, CTX),
        P(SMP, CTX, None),
        P(SMP, CTX, None),
    )
    return jax.shard_map(local, mesh=split, in_specs=in_specs, out_specs=out_specs, check_vma=False)
```

```python
import jax
import jax.numpy as jnp
from jax import lax
from jax.experimental import pallas as pl
from jax.experimental.pallas import tpu as pltpu
from jax.sharding import Mesh, PartitionSpec as P

CTX = ("z", "yh")
SMP = ("x", "yl", "core")
HEAD_DIM = 64
STATE = 128
BLOCK = 256
HEADS_DEV = 4
WIDTH = HEADS_DEV * HEAD_DIM
LANES = 128
F32 = jnp.float32
BF16 = jnp.bfloat16
VMEM_LIMIT = 60 * 1024 * 1024
SMALL_LIMIT = 24 * 1024 * 1024
STEP_BLOCKS = 4
CARRY_BLOCKS = 4


def iota(shape, dim):
    return lax.broadcasted_iota(jnp.int32, shape, dim)


def dot(a, b, dims=((1,), (0,))):
    return lax.dot_general(a, b, (dims, ((), ())), preferred_element_type=F32)


def split3(v):
    first = v.astype(BF16)
    rest = v - first.astype(F32)
    second = rest.astype(BF16)
    third = (rest - second.astype(F32)).astype(BF16)
    return first, second, third


def split2(v):
    first = v.astype(BF16)
    return first, (v - first.astype(F32)).astype(BF16)


def running_sums(logs):
    upper = (iota((BLOCK, BLOCK), 0) <= iota((BLOCK, BLOCK), 1)).astype(BF16)
    parts = []
    for at in range(0, logs.shape[1], BLOCK):
        parts += [logs[:, at : at + BLOCK]] * 2
    one, two, three = split3(jnp.concatenate(parts, axis=0))
    return dot(one, upper) + dot(two, upper) + dot(three, upper)


def columns(rows):
    cols = rows.T
    return [jnp.broadcast_to(cols[:, h : h + 1], (BLOCK, LANES)) for h in range(HEADS_DEV)]


def by_channel(spread):
    low = iota((BLOCK, LANES), 1) < HEAD_DIM
    return jnp.concatenate(
        [jnp.where(low, spread[0], spread[1]), jnp.where(low, spread[2], spread[3])], axis=1
    )


def spread_pieces(state, k):
    return state[:, k * LANES : (k + 1) * LANES].reshape(16, 8, LANES)


def carry_kernel(dy_ref, c_ref, logs_ref, rows_ref, r_ref, cum_ref, first_ref, r_scr, d_scr):
    step = pl.program_id(0)

    @pl.when(step == 0)
    def _():
        r_scr[...] = jnp.zeros_like(r_scr)
        d_scr[...] = jnp.ones_like(d_scr)
        rows_ref[...] = running_sums(logs_ref[...]).reshape(rows_ref.shape)

    last = pl.num_programs(0) - 1
    grad, dec = r_scr[...], d_scr[...]
    for j in range(CARRY_BLOCKS - 1, -1, -1):
        part = slice(j * BLOCK, (j + 1) * BLOCK)
        run = by_channel(columns(rows_ref[(last - step) * CARRY_BLOCKS + j]))
        high, low = split2(dy_ref[part].astype(F32) * jnp.exp(run))
        turned = c_ref[part].T
        final = jnp.exp(run[BLOCK - 1 : BLOCK])
        r_ref[j] = grad
        cum_ref[j] = dec
        grad = final * grad + (dot(turned, high) + dot(turned, low))
        dec = final * dec
    r_scr[...], d_scr[...] = grad, dec

    @pl.when(step == last)
    def _():
        for k in range(2):
            first_ref[:, k] = spread_pieces(grad, k)
        if first_ref.shape[1] > 2:
            both = jnp.concatenate([dec[0:4, :LANES], dec[0:4, LANES:]], axis=0)
            first_ref[:, 2] = jnp.broadcast_to(both[None], (16, 8, LANES))


def cost(passes, moved):
    return pl.CostEstimate(flops=passes * 2 * BLOCK**3, bytes_accessed=moved, transcendentals=0)


def carry(dy, c, logs, tiles):
    blocks = dy.shape[0] // BLOCK
    steps = blocks // CARRY_BLOCKS
    span = CARRY_BLOCKS * BLOCK
    back = lambda i: (steps - 1 - i, 0)
    back3 = lambda i: (steps - 1 - i, 0, 0)
    return pl.pallas_call(
        carry_kernel,
        grid=(steps,),
        in_specs=[
            pl.BlockSpec((span, WIDTH), back),
            pl.BlockSpec((span, STATE), back),
            whole_spec(HEADS_DEV, blocks * BLOCK),
        ],
        out_specs=[
            whole_spec(blocks, 8, BLOCK),
            pl.BlockSpec((CARRY_BLOCKS, STATE, WIDTH), back3),
            pl.BlockSpec((CARRY_BLOCKS, 8, WIDTH), back3),
            whole_spec(16, tiles, 8, LANES),
        ],
        out_shape=[
            jax.ShapeDtypeStruct((blocks, 8, BLOCK), F32),
            jax.ShapeDtypeStruct((blocks, STATE, WIDTH), F32),
            jax.ShapeDtypeStruct((blocks, 8, WIDTH), F32),
            jax.ShapeDtypeStruct((16, tiles, 8, LANES), F32),
        ],
        scratch_shapes=[pltpu.VMEM((STATE, WIDTH), F32), pltpu.VMEM((8, WIDTH), F32)],
        compiler_params=pltpu.CompilerParams(vmem_limit_bytes=VMEM_LIMIT),
        cost_estimate=cost(32, 3 * 2**20),
    )(dy, c, logs)


def load_state(s0_ref, m_scr):
    for r in range(64):
        m_scr[4 * r : 4 * r + 4] = s0_ref[:, LANES * r : LANES * (r + 1)]
    low = iota((64, LANES), 1) < HEAD_DIM
    halves = []
    for k in range(2):
        one = m_scr[pl.ds(2 * k, 64, stride=4), :]
        two = m_scr[pl.ds(2 * k + 1, 64, stride=4), :]
        even = jnp.where(low, one, pltpu.roll(two, HEAD_DIM, 1))
        odd = jnp.where(low, pltpu.roll(one, HEAD_DIM, 1), two)
        halves.append(jnp.concatenate([even, odd], axis=0))
    parted = jnp.concatenate(halves, axis=1)
    row, col = iota((STATE, STATE), 0), iota((STATE, STATE), 1)
    order = (col == (row & 1) * 64 + (row >> 1)).astype(BF16)
    one, two, three = split3(parted)
    return dot(order, one) + dot(order, two) + dot(order, three)


def weights(rows, spread):
    half = BLOCK // 2
    keep = iota((half, half), 1) >= iota((half, half), 0)
    out = []
    for h in range(HEADS_DEV):
        row = rows[h : h + 1]
        top, bottom = spread[h][:half], spread[h][half:]
        left = jnp.where(keep, jnp.exp(row[:, :half] - top), 0.0)
        right = jnp.exp(row[:, half:] - top)
        w_bot = jnp.where(keep, jnp.exp(row[:, half:] - bottom), 0.0)
        out.append((jnp.concatenate([left, right], axis=1), w_bot))
    return out


def proj_grads(x, dy, b, c, rows, r_in, state):
    half = BLOCK // 2
    spread = columns(rows)
    run = by_channel(spread)
    final = run[BLOCK - 1 : BLOCK]
    x_high, x_low = split2(x.astype(F32) * jnp.exp(final - run))
    dy_high, dy_low = split2(dy.astype(F32) * jnp.exp(run))
    r_both = jnp.concatenate(split2(r_in), axis=0)
    s_both = jnp.concatenate(split2(state), axis=0)
    turned = b.T
    after = jnp.exp(final) * state + (dot(turned, x_high) + dot(turned, x_low))

    lane_half = iota((BLOCK, LANES), 1)
    sum_top = jnp.zeros((half, BLOCK), F32)
    sum_bot = jnp.zeros((half, half), F32)
    for h, (w_top, w_bot) in enumerate(weights(rows, spread)):
        pair = slice((h // 2) * LANES, (h // 2 + 1) * LANES)
        mine = (lane_half < HEAD_DIM) if h % 2 == 0 else (lane_half >= HEAD_DIM)
        x_h = jnp.where(mine, x[:, pair], jnp.zeros((), BF16))
        dy_pair = dy[:, pair]
        sum_top = sum_top + w_top * dot(x_h[:half], dy_pair, ((1,), (1,)))
        sum_bot = sum_bot + w_bot * dot(x_h[half:], dy_pair[half:], ((1,), (1,)))
    w_top = sum_top.astype(BF16)
    w_bot = sum_bot.astype(BF16)
    b_state = dot(x_high, r_both, ((1,), (1,)))
    b_state = b_state[:, :STATE] + b_state[:, STATE:] + dot(x_low, r_both[:STATE], ((1,), (1,)))
    c_state = dot(dy_high, s_both, ((1,), (1,)))
    c_state = c_state[:, :STATE] + c_state[:, STATE:] + dot(dy_low, s_both[:STATE], ((1,), (1,)))
    b_top = b_state[:half] + dot(w_top, c)
    b_bot = b_state[half:] + dot(w_bot, c[half:])
    c_top = c_state[:half] + dot(w_top[:, :half], b[:half], ((0,), (0,)))
    c_bot = (
        c_state[half:]
        + dot(w_top[:, half:], b[:half], ((0,), (0,)))
        + dot(w_bot, b[half:], ((0,), (0,)))
    )
    return after, b_top, b_bot, c_top, c_bot


def input_grads(dy, b, c, rows, r_in):
    half = BLOCK // 2
    spread = columns(rows)
    run = by_channel(spread)
    to_end = jnp.exp(run[BLOCK - 1 : BLOCK] - run)
    r_both = jnp.concatenate(split2(r_in), axis=0)
    bc_top = dot(b[:half], c, ((1,), (1,)))
    bc_bot = dot(b[half:], c[half:], ((1,), (1,)))
    lane = iota((BLOCK, WIDTH), 1)
    coeff_top, coeff_bot, dy_top, dy_bot = [], [], [], []
    for h, (w_top, w_bot) in enumerate(weights(rows, spread)):
        mine = (lane >= h * HEAD_DIM) & (lane < (h + 1) * HEAD_DIM)
        dy_h = jnp.where(mine, dy, jnp.zeros((), BF16))
        coeff_top.append((w_top * bc_top).astype(BF16))
        coeff_bot.append((w_bot * bc_bot).astype(BF16))
        dy_top.append(dy_h)
        dy_bot.append(dy_h[half:])
    from_r = to_end * dot(jnp.concatenate([b, b], axis=1), r_both)
    top = from_r[:half] + dot(jnp.concatenate(coeff_top, axis=1), jnp.concatenate(dy_top, axis=0))
    bottom = from_r[half:] + dot(jnp.concatenate(coeff_bot, axis=1), jnp.concatenate(dy_bot, axis=0))
    return top, bottom


def each_block(x_ref, dy_ref, b_ref, c_ref, rows_ref, r_ref, s0_ref, s_scr, m_scr):
    @pl.when(pl.program_id(0) == 0)
    def _():
        s_scr[...] = load_state(s0_ref, m_scr)

    state = s_scr[...]
    for j in range(STEP_BLOCKS):
        at = j * BLOCK
        part = slice(at, at + BLOCK)
        state, *grads = proj_grads(
            x_ref[part], dy_ref[part], b_ref[part], c_ref[part], rows_ref[j], r_ref[j], state
        )
        yield j, at, grads
    s_scr[...] = state


def answer_kernel(
    x_ref, dy_ref, b_ref, c_ref, rows_ref, r_ref, s0_ref, after_ref, bc_ref, s_scr, m_scr
):
    refs = (x_ref, dy_ref, b_ref, c_ref, rows_ref, r_ref, s0_ref, s_scr, m_scr)
    for j, _, (b_top, b_bot, c_top, c_bot) in each_block(*refs):
        bc_ref[2 * j, 0:LANES] = b_top
        bc_ref[2 * j, LANES:] = c_top
        bc_ref[2 * j + 1, 0:LANES] = b_bot
        bc_ref[2 * j + 1, LANES:] = c_bot


def prompt_kernel(
    x_ref, dy_ref, b_ref, c_ref, rows_ref, r_ref, s0_ref, core_ref, after_ref,
    b_out_ref, keep_ref, send_ref, s_scr, m_scr,
):
    first = core_ref[0] == 0
    refs = (x_ref, dy_ref, b_ref, c_ref, rows_ref, r_ref, s0_ref, s_scr, m_scr)
    for j, at, (b_top, b_bot, c_top, c_bot) in each_block(*refs):
        b_out_ref[at : at + LANES] = b_top
        b_out_ref[at + LANES : at + BLOCK] = b_bot
        keep_ref[j] = jnp.where(first, c_top, c_bot)
        send_ref[j] = jnp.where(first, c_bot, c_top)


def finish_kernel(
    x_ref, rows_ref, cum_ref, b_in_ref, enter_ref, core_ref, c_keep_ref, c_got_ref, after_ref, keep_ref, send_ref, g_scr
):
    @pl.when(pl.program_id(0) == 0)
    def _():
        for k in range(2):
            high, low = split2(enter_ref[:, k].reshape(STATE, LANES))
            g_scr[:STATE, k * LANES : (k + 1) * LANES] = high
            g_scr[STATE:, k * LANES : (k + 1) * LANES] = low

    first = core_ref[0] == 0
    g_both = g_scr[...]
    for j in range(STEP_BLOCKS):
        part = slice(j * BLOCK, (j + 1) * BLOCK)
        run = by_channel(columns(rows_ref[j]))
        to_end = jnp.exp(run[BLOCK - 1 : BLOCK] - run) * cum_ref[j, 0:1]
        high, low = split2(x_ref[part].astype(F32) * to_end)
        fresh = dot(high, g_both, ((1,), (1,)))
        fresh = fresh[:, :STATE] + fresh[:, STATE:] + dot(low, g_both[:STATE], ((1,), (1,)))
        total = b_in_ref[part] + fresh
        keep_ref[j, 0:LANES] = jnp.where(first, total[:LANES], total[LANES:])
        keep_ref[j, LANES:] = c_keep_ref[j] + c_got_ref[j]
        send_ref[j] = jnp.where(first, total[LANES:], total[:LANES])


def merge_kernel(keep_ref, got_ref, out_ref):
    out_ref[...] = keep_ref[...] + got_ref[...]


def answer_x_kernel(dy_ref, b_ref, c_ref, rows_ref, r_ref, after_ref, gx_ref):
    for j in range(STEP_BLOCKS):
        at = j * BLOCK
        part = slice(at, at + BLOCK)
        top, bottom = input_grads(dy_ref[part], b_ref[part], c_ref[part], rows_ref[j], r_ref[j])
        gx_ref[at : at + LANES] = top
        gx_ref[at + LANES : at + BLOCK] = bottom


def prompt_x_kernel(dy_ref, b_ref, c_ref, rows_ref, r_ref, cum_ref, enter_ref, after_ref, gx_ref, g_scr):
    @pl.when(pl.program_id(0) == 0)
    def _():
        for k in range(2):
            g_scr[:, k * LANES : (k + 1) * LANES] = enter_ref[:, k].reshape(STATE, LANES)

    for j in range(STEP_BLOCKS):
        at = j * BLOCK
        part = slice(at, at + BLOCK)
        r_in = r_ref[j] + cum_ref[j, 0:1] * g_scr[...]
        top, bottom = input_grads(dy_ref[part], b_ref[part], c_ref[part], rows_ref[j], r_in)
        gx_ref[at : at + LANES] = top
        gx_ref[at + LANES : at + BLOCK] = bottom


SPAN = STEP_BLOCKS * BLOCK


def tall_spec(width):
    return pl.BlockSpec((SPAN, width), lambda i: (i, 0))


def block_spec(*shape):
    return pl.BlockSpec((STEP_BLOCKS,) + shape, lambda i: (i,) + (0,) * len(shape))


def whole_spec(*shape):
    return pl.BlockSpec(shape, lambda i: (0,) * len(shape))


ROWS = block_spec(8, BLOCK)
STATES = block_spec(STATE, WIDTH)
DECAYS = block_spec(8, WIDTH)
ENTERING = whole_spec(16, 2, 8, LANES)
SCALAR = pl.BlockSpec(memory_space=pltpu.SMEM)
ORDER = pl.BlockSpec(memory_space=pl.ANY)


def call(kernel, in_specs, out_specs, out_shape, scratch, passes, args, limit=VMEM_LIMIT):
    return pl.pallas_call(
        kernel,
        grid=(args[0].shape[0] // SPAN,),
        in_specs=in_specs,
        out_specs=out_specs,
        out_shape=[jax.ShapeDtypeStruct(shape, F32) for shape in out_shape],
        scratch_shapes=[pltpu.VMEM(shape, kind) for shape, kind in scratch],
        compiler_params=pltpu.CompilerParams(vmem_limit_bytes=limit),
        cost_estimate=cost(passes, 6 * 2**20),
    )(*args)


MAIN = [tall_spec(WIDTH), tall_spec(WIDTH), tall_spec(STATE), tall_spec(STATE), ROWS, STATES]
MAIN += [whole_spec(HEADS_DEV, STATE * HEAD_DIM)]
MAIN_SCRATCH = [((STATE, WIDTH), F32), ((256, LANES), F32)]


def answer_call(*args):
    chunks = args[0].shape[0] // LANES
    out = pl.BlockSpec((2 * STEP_BLOCKS, BLOCK, LANES), lambda i: (i, 0, 0))
    return call(answer_kernel, MAIN + [ORDER], [out], [(chunks, BLOCK, LANES)], MAIN_SCRATCH, 96, args)[0]


def prompt_call(*args):
    length = args[0].shape[0]
    half = (length // BLOCK, LANES, LANES)
    specs = [tall_spec(STATE), block_spec(LANES, LANES), block_spec(LANES, LANES)]
    shapes = [(length, STATE), half, half]
    return call(prompt_kernel, MAIN + [SCALAR, ORDER], specs, shapes, MAIN_SCRATCH, 96, args)


def finish_call(*args):
    blocks = args[0].shape[0] // BLOCK
    half = block_spec(LANES, LANES)
    specs = [tall_spec(WIDTH), ROWS, DECAYS, tall_spec(STATE), ENTERING, SCALAR, half, half, ORDER]
    outs = [block_spec(BLOCK, LANES), half]
    shapes = [(blocks, BLOCK, LANES), (blocks, LANES, LANES)]
    scratch = [((2 * STATE, WIDTH), BF16)]
    return call(finish_kernel, specs, outs, shapes, scratch, 32, args, SMALL_LIMIT)


def merge_call(keep, got):
    spec = pl.BlockSpec(got.shape, lambda i: (0, 0, 0))
    return pl.pallas_call(
        merge_kernel,
        grid=(1,),
        in_specs=[spec, spec],
        out_specs=spec,
        out_shape=jax.ShapeDtypeStruct(keep.shape, F32),
        input_output_aliases={0: 0},
        compiler_params=pltpu.CompilerParams(vmem_limit_bytes=SMALL_LIMIT),
    )(keep, got)


INPUT = [tall_spec(WIDTH), tall_spec(STATE), tall_spec(STATE), ROWS, STATES]


def answer_x_call(*args):
    out = [args[0].shape]
    return call(answer_x_kernel, INPUT + [ORDER], [tall_spec(WIDTH)], out, [], 80, args)[0]


def prompt_x_call(*args):
    out = [args[0].shape]
    specs = INPUT + [DECAYS, ENTERING, ORDER]
    scratch = [((STATE, WIDTH), F32)]
    return call(prompt_x_kernel, specs, [tall_spec(WIDTH)], out, scratch, 80, args)[0]


def scan_kernel(in_ref, out_ref):
    for k in range(2):
        grad = in_ref[0, 3 + k]
        for a in range(1, 16):
            grad = grad + in_ref[a, 3 + k]
        for j in range(15, -1, -1):
            out_ref[j, k] = grad
            grad = in_ref[j, k] + in_ref[j, 2, 4 * k : 4 * k + 1] * grad


def scan_call(pieces):
    return pl.pallas_call(
        scan_kernel,
        out_shape=jax.ShapeDtypeStruct((16, 2, 8, LANES), F32),
        compiler_params=pltpu.CompilerParams(vmem_limit_bytes=SMALL_LIMIT),
    )(pieces)


def swap(v, axis):
    return lax.all_to_all(v, axis, 0, 0, tiled=True)


def local(
    prompt_inputs,
    prompt_outgrad,
    prompt_bproj,
    prompt_cproj,
    prompt_decay,
    prompt_states,
    answer_inputs,
    answer_outgrad,
    answer_bproj,
    answer_cproj,
    answer_decay,
    answer_state,
):
    core = lax.axis_index("core").astype(jnp.int32)[None]
    side = lax.axis_index("yh")
    other = [(0, 1), (1, 0)]
    turn = [(c * 16 + s, s * 16 + c) for c in range(16) for s in range(16)]
    a_x, a_dy, a_b, a_c = answer_inputs[0], answer_outgrad[0], answer_bproj[0], answer_cproj[0]

    a_rows, a_r, _, a_first = carry(a_dy, a_c, answer_decay[0], 2)
    a_turned = lax.ppermute(a_first, CTX + SMP, turn)
    p_rows, p_r, p_cum, p_first = carry(prompt_outgrad, prompt_cproj, prompt_decay, 3)
    answer_bc = answer_call(a_x, a_dy, a_b, a_c, a_rows, a_r, answer_state, p_first)
    a_turned, answer_bc = lax.optimization_barrier((a_turned, answer_bc))
    answer_part = lax.psum_scatter(answer_bc, "z", scatter_dimension=0, tiled=True)
    shards = swap(jnp.concatenate([p_first, a_turned], axis=1), CTX)
    prompt_b, c_keep, c_send = prompt_call(
        prompt_inputs,
        prompt_outgrad,
        prompt_bproj,
        prompt_cproj,
        p_rows,
        p_r,
        prompt_states[0],
        core,
        answer_bc,
    )
    grads, c_send, c_keep = lax.optimization_barrier((scan_call(shards), c_send, c_keep))
    entering = swap(grads, CTX)
    c_got = lax.ppermute(c_send, "core", other)
    answer_gx = answer_x_call(a_dy, a_b, a_c, a_rows, a_r, grads)
    b_keep, b_send = finish_call(
        prompt_inputs, p_rows, p_cum, prompt_b, entering, core, c_keep, c_got, answer_gx
    )
    b_got = lax.ppermute(b_send, "core", other)
    chip = merge_call(b_keep, b_got)
    answer_send = lax.dynamic_index_in_dim(answer_part, 1 - side, 0)
    answer_keep = lax.dynamic_index_in_dim(answer_part, side, 0)
    chip, answer_send, answer_keep = lax.optimization_barrier((chip, answer_send, answer_keep))
    prompt_sum = jnp.sum(swap(chip, ("x", "yl")), axis=0)
    prompt_gx = prompt_x_call(
        prompt_outgrad, prompt_bproj, prompt_cproj, p_rows, p_r, p_cum, entering, b_send
    )
    answer_sum = answer_keep + lax.ppermute(answer_send, "yh", other)
    return (
        prompt_gx,
        prompt_sum[:LANES],
        prompt_sum[LANES:],
        answer_gx[None],
        answer_sum[:, :LANES],
        answer_sum[:, LANES:],
    )


def solution(mesh):
    split = Mesh(mesh.devices.reshape(8, 2, 4, 2, 2), CTX + SMP)
    in_specs = (
        P(CTX, SMP),
        P(CTX, SMP),
        P(CTX, None),
        P(CTX, None),
        P(SMP, CTX),
        P(CTX, SMP, None),
        P(SMP, None, CTX),
        P(SMP, None, CTX),
        P(SMP, None, None),
        P(SMP, None, None),
        P(SMP, CTX, None),
        P(CTX, None),
    )
    out_specs = (
        P(CTX, SMP),
        P(CTX + SMP, None),
        P(CTX + SMP, None),
        P(SMP, None, CTX),
        P(SMP, CTX, None),
        P(SMP, CTX, None),
    )
    return jax.shard_map(local, mesh=split, in_specs=in_specs, out_specs=out_specs, check_vma=False)
```

```python
import jax
import jax.numpy as jnp
from jax import lax
from jax.experimental import pallas as pl
from jax.experimental.pallas import tpu as pltpu
from jax.sharding import Mesh, PartitionSpec as P

CTX = ("z", "yh")
SMP = ("x", "yl", "core")
HEAD_DIM = 64
STATE = 128
BLOCK = 256
HEADS_DEV = 4
WIDTH = HEADS_DEV * HEAD_DIM
LANES = 128
F32 = jnp.float32
BF16 = jnp.bfloat16
SHIFTS = ((0, 0), (2, 1), (1, 1), (3, 1), (0, 1), (2, 0), (1, 0), (3, 0))
LOG2E = 1.4426950408889634
VMEM_LIMIT = 60 * 1024 * 1024
SMALL_LIMIT = 24 * 1024 * 1024
STEP_BLOCKS = 4
CARRY_BLOCKS = 4


def iota(shape, dim):
    return lax.broadcasted_iota(jnp.int32, shape, dim)


def dot(a, b, dims=((1,), (0,))):
    return lax.dot_general(a, b, (dims, ((), ())), preferred_element_type=F32)


def split3(v):
    first = v.astype(BF16)
    rest = v - first.astype(F32)
    second = rest.astype(BF16)
    third = (rest - second.astype(F32)).astype(BF16)
    return first, second, third


def split2(v):
    first = v.astype(BF16)
    return first, (v - first.astype(F32)).astype(BF16)


def running_sums(logs):
    upper = (iota((BLOCK, BLOCK), 0) <= iota((BLOCK, BLOCK), 1)).astype(BF16)
    logs = logs * LOG2E
    parts = []
    for at in range(0, logs.shape[1], BLOCK):
        parts += [logs[:, at : at + BLOCK]] * 2
    one, two, three = split3(jnp.concatenate(parts, axis=0))
    return dot(one, upper) + dot(two, upper) + dot(three, upper)


def expand(rows, width):
    first = rows.astype(BF16).astype(F32)
    rest = rows - first
    second = rest.astype(BF16).astype(F32)
    parts = jnp.concatenate([first, second, rest - second, jnp.zeros_like(rows)], axis=0).astype(BF16)
    shape = (32, HEADS_DEV * width)
    lane = iota(shape, 1)
    pick = (iota(shape, 0) & 7) * width
    mine = ((lane >= pick) & (lane < pick + width)).astype(BF16)
    return dot(parts, mine, ((0,), (0,)))


def from_start(rows):
    return expand(jnp.exp2(rows), HEAD_DIM)


def to_end(rows):
    return expand(jnp.exp2(rows[:, BLOCK - 1 : BLOCK] - rows), HEAD_DIM)


def per_head(rows):
    spread = expand(rows, LANES)
    return [spread[:, h * LANES : (h + 1) * LANES] for h in range(HEADS_DEV)]


def spread_pieces(state, k):
    return state[:, k * LANES : (k + 1) * LANES].reshape(16, 8, LANES)


def carry_kernel(dy_ref, c_ref, logs_ref, rows_ref, r_ref, cum_ref, first_ref, r_scr, d_scr):
    step = pl.program_id(0)

    @pl.when(step == 0)
    def _():
        r_scr[...] = jnp.zeros_like(r_scr)
        d_scr[...] = jnp.ones_like(d_scr)
        rows_ref[...] = running_sums(logs_ref[...]).reshape(rows_ref.shape)

    last = pl.num_programs(0) - 1
    grad, dec = r_scr[...], d_scr[...]
    for j in range(CARRY_BLOCKS - 1, -1, -1):
        part = slice(j * BLOCK, (j + 1) * BLOCK)
        start = from_start(rows_ref[(last - step) * CARRY_BLOCKS + j])
        high, low = split2(dy_ref[part].astype(F32) * start)
        turned = c_ref[part].T
        final = start[BLOCK - 1 : BLOCK]
        r_ref[j] = grad
        cum_ref[j] = dec
        grad = final * grad + (dot(turned, high) + dot(turned, low))
        dec = final * dec
    r_scr[...], d_scr[...] = grad, dec

    @pl.when(step == last)
    def _():
        for k in range(2):
            first_ref[:, k] = spread_pieces(grad, k)
        if first_ref.shape[1] > 2:
            both = jnp.concatenate([dec[0:4, :LANES], dec[0:4, LANES:]], axis=0)
            first_ref[:, 2] = jnp.broadcast_to(both[None], (16, 8, LANES))


def cost(passes, moved):
    return pl.CostEstimate(flops=passes * 2 * BLOCK**3, bytes_accessed=moved, transcendentals=0)


def carry(dy, c, logs, tiles):
    blocks = dy.shape[0] // BLOCK
    steps = blocks // CARRY_BLOCKS
    span = CARRY_BLOCKS * BLOCK
    back = lambda i: (steps - 1 - i, 0)
    back3 = lambda i: (steps - 1 - i, 0, 0)
    return pl.pallas_call(
        carry_kernel,
        grid=(steps,),
        in_specs=[
            pl.BlockSpec((span, WIDTH), back),
            pl.BlockSpec((span, STATE), back),
            whole_spec(HEADS_DEV, blocks * BLOCK),
        ],
        out_specs=[
            whole_spec(blocks, 8, BLOCK),
            pl.BlockSpec((CARRY_BLOCKS, STATE, WIDTH), back3),
            pl.BlockSpec((CARRY_BLOCKS, 8, WIDTH), back3),
            whole_spec(16, tiles, 8, LANES),
        ],
        out_shape=[
            jax.ShapeDtypeStruct((blocks, 8, BLOCK), F32),
            jax.ShapeDtypeStruct((blocks, STATE, WIDTH), F32),
            jax.ShapeDtypeStruct((blocks, 8, WIDTH), F32),
            jax.ShapeDtypeStruct((16, tiles, 8, LANES), F32),
        ],
        scratch_shapes=[pltpu.VMEM((STATE, WIDTH), F32), pltpu.VMEM((8, WIDTH), F32)],
        compiler_params=pltpu.CompilerParams(vmem_limit_bytes=VMEM_LIMIT),
        cost_estimate=cost(32, 3 * 2**20),
    )(dy, c, logs)


def load_state(s0_ref, m_scr):
    for r in range(64):
        m_scr[4 * r : 4 * r + 4] = s0_ref[:, LANES * r : LANES * (r + 1)]
    low = iota((64, LANES), 1) < HEAD_DIM
    halves = []
    for k in range(2):
        one = m_scr[pl.ds(2 * k, 64, stride=4), :]
        two = m_scr[pl.ds(2 * k + 1, 64, stride=4), :]
        even = jnp.where(low, one, pltpu.roll(two, HEAD_DIM, 1))
        odd = jnp.where(low, pltpu.roll(one, HEAD_DIM, 1), two)
        halves.append(jnp.concatenate([even, odd], axis=0))
    parted = jnp.concatenate(halves, axis=1)
    row, col = iota((STATE, STATE), 0), iota((STATE, STATE), 1)
    order = (col == (row & 1) * 64 + (row >> 1)).astype(BF16)
    one, two, three = split3(parted)
    return dot(order, one) + dot(order, two) + dot(order, three)


def weights(rows, spread):
    half = BLOCK // 2
    keep = iota((half, half), 1) >= iota((half, half), 0)
    out = []
    for h in range(HEADS_DEV):
        row = rows[h : h + 1]
        top, bottom = spread[h][:half], spread[h][half:]
        left = jnp.where(keep, jnp.exp2(row[:, :half] - top), 0.0)
        right = jnp.exp2(row[:, half:] - top)
        w_bot = jnp.where(keep, jnp.exp2(row[:, half:] - bottom), 0.0)
        out.append((jnp.concatenate([left, right], axis=1), w_bot))
    return out


def proj_grads(x, dy, b, c, rows, r_in, state):
    half = BLOCK // 2
    cols = rows.T
    spread = [jnp.broadcast_to(cols[:, h : h + 1], (BLOCK, LANES)) for h in range(HEADS_DEV)]
    left = iota((BLOCK, LANES), 1) < HEAD_DIM
    run = jnp.concatenate(
        [jnp.where(left, spread[0], spread[1]), jnp.where(left, spread[2], spread[3])], axis=1
    )
    start = jnp.exp2(run)
    x_high, x_low = split2(x.astype(F32) * jnp.exp2(run[BLOCK - 1 : BLOCK] - run))
    dy_high, dy_low = split2(dy.astype(F32) * start)
    r_both = jnp.concatenate(split2(r_in), axis=0)
    s_both = jnp.concatenate(split2(state), axis=0)
    turned = b.T
    after = start[BLOCK - 1 : BLOCK] * state + (dot(turned, x_high) + dot(turned, x_low))

    lane_half = iota((BLOCK, LANES), 1)
    sum_top = jnp.zeros((half, BLOCK), F32)
    sum_bot = jnp.zeros((half, half), F32)
    for h, (w_top, w_bot) in enumerate(weights(rows, spread)):
        pair = slice((h // 2) * LANES, (h // 2 + 1) * LANES)
        mine = (lane_half < HEAD_DIM) if h % 2 == 0 else (lane_half >= HEAD_DIM)
        x_h = jnp.where(mine, x[:, pair], jnp.zeros((), BF16))
        dy_pair = dy[:, pair]
        sum_top = sum_top + w_top * dot(x_h[:half], dy_pair, ((1,), (1,)))
        sum_bot = sum_bot + w_bot * dot(x_h[half:], dy_pair[half:], ((1,), (1,)))
    w_top = sum_top.astype(BF16)
    w_bot = sum_bot.astype(BF16)
    b_state = dot(x_high, r_both, ((1,), (1,)))
    b_state = b_state[:, :STATE] + b_state[:, STATE:] + dot(x_low, r_both[:STATE], ((1,), (1,)))
    c_state = dot(dy_high, s_both, ((1,), (1,)))
    c_state = c_state[:, :STATE] + c_state[:, STATE:] + dot(dy_low, s_both[:STATE], ((1,), (1,)))
    b_top = b_state[:half] + dot(w_top, c)
    b_bot = b_state[half:] + dot(w_bot, c[half:])
    c_top = c_state[:half] + dot(w_top[:, :half], b[:half], ((0,), (0,)))
    c_bot = (
        c_state[half:]
        + dot(w_top[:, half:], b[:half], ((0,), (0,)))
        + dot(w_bot, b[half:], ((0,), (0,)))
    )
    return after, b_top, b_bot, c_top, c_bot


def input_grads(dy, b, c, rows, r_in):
    half = BLOCK // 2
    spread = per_head(rows)
    r_both = jnp.concatenate(split2(r_in), axis=0)
    bc_top = dot(b[:half], c, ((1,), (1,)))
    bc_bot = dot(b[half:], c[half:], ((1,), (1,)))
    lane = iota((BLOCK, WIDTH), 1)
    coeff_top, coeff_bot, dy_top, dy_bot = [], [], [], []
    for h, (w_top, w_bot) in enumerate(weights(rows, spread)):
        mine = (lane >= h * HEAD_DIM) & (lane < (h + 1) * HEAD_DIM)
        dy_h = jnp.where(mine, dy, jnp.zeros((), BF16))
        coeff_top.append((w_top * bc_top).astype(BF16))
        coeff_bot.append((w_bot * bc_bot).astype(BF16))
        dy_top.append(dy_h)
        dy_bot.append(dy_h[half:])
    from_r = to_end(rows) * dot(jnp.concatenate([b, b], axis=1), r_both)
    top = from_r[:half] + dot(jnp.concatenate(coeff_top, axis=1), jnp.concatenate(dy_top, axis=0))
    bottom = from_r[half:] + dot(jnp.concatenate(coeff_bot, axis=1), jnp.concatenate(dy_bot, axis=0))
    return top, bottom


def each_block(x_ref, dy_ref, b_ref, c_ref, rows_ref, r_ref, s0_ref, s_scr, m_scr):
    @pl.when(pl.program_id(0) == 0)
    def _():
        s_scr[...] = load_state(s0_ref, m_scr)

    state = s_scr[...]
    for j in range(STEP_BLOCKS):
        at = j * BLOCK
        part = slice(at, at + BLOCK)
        state, *grads = proj_grads(
            x_ref[part], dy_ref[part], b_ref[part], c_ref[part], rows_ref[j], r_ref[j], state
        )
        yield j, at, grads
    s_scr[...] = state


def answer_kernel(
    x_ref, dy_ref, b_ref, c_ref, rows_ref, r_ref, s0_ref, side_ref, after_ref, keep_ref, send_ref, s_scr, m_scr
):
    first = side_ref[0] == 0
    refs = (x_ref, dy_ref, b_ref, c_ref, rows_ref, r_ref, s0_ref, s_scr, m_scr)
    for j, _, (b_top, b_bot, c_top, c_bot) in each_block(*refs):
        keep_ref[j, 0:LANES] = jnp.where(first, b_top, b_bot)
        keep_ref[j, LANES:] = jnp.where(first, c_top, c_bot)
        send_ref[j, 0:LANES] = jnp.where(first, b_bot, b_top)
        send_ref[j, LANES:] = jnp.where(first, c_bot, c_top)


def prompt_kernel(
    x_ref, dy_ref, b_ref, c_ref, rows_ref, r_ref, s0_ref, core_ref, after_ref,
    b_out_ref, keep_ref, send_ref, s_scr, m_scr,
):
    first = core_ref[0] == 0
    refs = (x_ref, dy_ref, b_ref, c_ref, rows_ref, r_ref, s0_ref, s_scr, m_scr)
    for j, at, (b_top, b_bot, c_top, c_bot) in each_block(*refs):
        b_out_ref[at : at + LANES] = b_top
        b_out_ref[at + LANES : at + BLOCK] = b_bot
        keep_ref[j] = jnp.where(first, c_top, c_bot)
        send_ref[j] = jnp.where(first, c_bot, c_top)


def finish_kernel(
    x_ref, rows_ref, cum_ref, b_in_ref, enter_ref, core_ref, after_ref, keep_ref, send_ref, g_scr
):
    @pl.when(pl.program_id(0) == 0)
    def _():
        for k in range(2):
            high, low = split2(enter_ref[:, k].reshape(STATE, LANES))
            g_scr[:STATE, k * LANES : (k + 1) * LANES] = high
            g_scr[STATE:, k * LANES : (k + 1) * LANES] = low

    first = core_ref[0] == 0
    g_both = g_scr[...]
    for j in range(STEP_BLOCKS):
        part = slice(j * BLOCK, (j + 1) * BLOCK)
        scale = to_end(rows_ref[j]) * cum_ref[j, 0:1]
        high, low = split2(x_ref[part].astype(F32) * scale)
        fresh = dot(high, g_both, ((1,), (1,)))
        fresh = fresh[:, :STATE] + fresh[:, STATE:] + dot(low, g_both[:STATE], ((1,), (1,)))
        total = b_in_ref[part] + fresh
        keep_ref[j] = jnp.where(first, total[:LANES], total[LANES:])
        send_ref[j] = jnp.where(first, total[LANES:], total[:LANES])


def merge_kernel(keep_ref, got_ref, c_ref, x_ref, yl_ref, *out_refs):
    for out_ref, (dx, dy) in zip(out_refs, SHIFTS):
        to = ((x_ref[0] + dx) & 3) * 2 + (yl_ref[0] ^ dy)
        out_ref[0:LANES] = keep_ref[to] + got_ref[to]
        out_ref[LANES:] = c_ref[to]


def answer_x_kernel(
    dy_ref, b_ref, c_ref, rows_ref, r_ref, c_keep_ref, c_got_ref, after_ref, gx_ref, c_sum_ref
):
    c_sum_ref[...] = c_keep_ref[...] + c_got_ref[...]
    for j in range(STEP_BLOCKS):
        at = j * BLOCK
        part = slice(at, at + BLOCK)
        top, bottom = input_grads(dy_ref[part], b_ref[part], c_ref[part], rows_ref[j], r_ref[j])
        gx_ref[at : at + LANES] = top
        gx_ref[at + LANES : at + BLOCK] = bottom


def prompt_x_kernel(dy_ref, b_ref, c_ref, rows_ref, r_ref, cum_ref, enter_ref, after_ref, gx_ref, g_scr):
    @pl.when(pl.program_id(0) == 0)
    def _():
        for k in range(2):
            g_scr[:, k * LANES : (k + 1) * LANES] = enter_ref[:, k].reshape(STATE, LANES)

    for j in range(STEP_BLOCKS):
        at = j * BLOCK
        part = slice(at, at + BLOCK)
        r_in = r_ref[j] + cum_ref[j, 0:1] * g_scr[...]
        top, bottom = input_grads(dy_ref[part], b_ref[part], c_ref[part], rows_ref[j], r_in)
        gx_ref[at : at + LANES] = top
        gx_ref[at + LANES : at + BLOCK] = bottom


SPAN = STEP_BLOCKS * BLOCK


def tall_spec(width):
    return pl.BlockSpec((SPAN, width), lambda i: (i, 0))


def block_spec(*shape):
    return pl.BlockSpec((STEP_BLOCKS,) + shape, lambda i: (i,) + (0,) * len(shape))


def whole_spec(*shape):
    return pl.BlockSpec(shape, lambda i: (0,) * len(shape))


ROWS = block_spec(8, BLOCK)
STATES = block_spec(STATE, WIDTH)
DECAYS = block_spec(8, WIDTH)
ENTERING = whole_spec(16, 2, 8, LANES)
SCALAR = pl.BlockSpec(memory_space=pltpu.SMEM)
ORDER = pl.BlockSpec(memory_space=pl.ANY)


def call(kernel, in_specs, out_specs, out_shape, scratch, passes, args, limit=VMEM_LIMIT):
    return pl.pallas_call(
        kernel,
        grid=(args[0].shape[0] // SPAN,),
        in_specs=in_specs,
        out_specs=out_specs,
        out_shape=[jax.ShapeDtypeStruct(shape, F32) for shape in out_shape],
        scratch_shapes=[pltpu.VMEM(shape, kind) for shape, kind in scratch],
        compiler_params=pltpu.CompilerParams(vmem_limit_bytes=limit),
        cost_estimate=cost(passes, 6 * 2**20),
    )(*args)


MAIN = [tall_spec(WIDTH), tall_spec(WIDTH), tall_spec(STATE), tall_spec(STATE), ROWS, STATES]
MAIN += [whole_spec(HEADS_DEV, STATE * HEAD_DIM)]
MAIN_SCRATCH = [((STATE, WIDTH), F32), ((256, LANES), F32)]


def answer_call(*args):
    half = (args[0].shape[0] // BLOCK, BLOCK, LANES)
    specs = [block_spec(BLOCK, LANES)] * 2
    return call(answer_kernel, MAIN + [SCALAR, ORDER], specs, [half, half], MAIN_SCRATCH, 96, args)


def prompt_call(*args):
    length = args[0].shape[0]
    half = (length // BLOCK, LANES, LANES)
    specs = [tall_spec(STATE), block_spec(LANES, LANES), block_spec(LANES, LANES)]
    shapes = [(length, STATE), half, half]
    return call(prompt_kernel, MAIN + [SCALAR, ORDER], specs, shapes, MAIN_SCRATCH, 96, args)


def finish_call(*args):
    blocks = args[0].shape[0] // BLOCK
    half = block_spec(LANES, LANES)
    specs = [tall_spec(WIDTH), ROWS, DECAYS, tall_spec(STATE), ENTERING, SCALAR, ORDER]
    outs = [half, half]
    shapes = [(blocks, LANES, LANES), (blocks, LANES, LANES)]
    scratch = [((2 * STATE, WIDTH), BF16)]
    return call(finish_kernel, specs, outs, shapes, scratch, 32, args)


def merge_call(keep, got, c, x, yl):
    vmem = pl.BlockSpec(memory_space=pltpu.VMEM)
    return pl.pallas_call(
        merge_kernel,
        in_specs=[vmem, vmem, vmem, SCALAR, SCALAR],
        out_specs=[vmem] * len(SHIFTS),
        out_shape=[jax.ShapeDtypeStruct((BLOCK, LANES), F32)] * len(SHIFTS),
        compiler_params=pltpu.CompilerParams(vmem_limit_bytes=SMALL_LIMIT),
    )(keep, got, c, x, yl)


def shifted(parts):
    out = [parts[0]]
    for part, (dx, dy) in zip(parts[1:], SHIFTS[1:]):
        way = [(x * 2 + y, (x + dx) % 4 * 2 + (y ^ dy)) for x in range(4) for y in range(2)]
        out.append(lax.ppermute(part, ("x", "yl"), way))
    return out


def sums_kernel(z_ref, *refs):
    parts, (pb_ref, pc_ref, ab_ref, ac_ref) = refs[:-4], refs[-4:]
    prompt = parts[0][...]
    for part in parts[1:]:
        prompt = prompt + part[...]
    answer = z_ref[0]
    for k in range(1, z_ref.shape[0]):
        answer = answer + z_ref[k]
    pb_ref[...] = prompt[:LANES]
    pc_ref[...] = prompt[LANES:]
    ab_ref[...] = answer[:LANES]
    ac_ref[...] = answer[LANES:]


def sums_call(answer_parts, prompt_parts):
    return pl.pallas_call(
        sums_kernel,
        out_shape=[jax.ShapeDtypeStruct((LANES, LANES), F32)] * 4,
        compiler_params=pltpu.CompilerParams(vmem_limit_bytes=SMALL_LIMIT),
    )(answer_parts, *prompt_parts)


INPUT = [tall_spec(WIDTH), tall_spec(STATE), tall_spec(STATE), ROWS, STATES]


def answer_x_call(*args):
    half = block_spec(LANES, LANES)
    outs = [tall_spec(WIDTH), half]
    shapes = [args[0].shape, args[5].shape]
    return call(answer_x_kernel, INPUT + [half, half, ORDER], outs, shapes, [], 80, args)


def prompt_x_call(*args):
    out = [args[0].shape]
    specs = INPUT + [DECAYS, ENTERING, ORDER]
    scratch = [((STATE, WIDTH), F32)]
    return call(prompt_x_kernel, specs, [tall_spec(WIDTH)], out, scratch, 80, args)[0]


def scan_kernel(in_ref, out_ref):
    for k in range(2):
        grad = in_ref[0, 3 + k]
        for a in range(1, 16):
            grad = grad + in_ref[a, 3 + k]
        for j in range(15, -1, -1):
            out_ref[j, k] = grad
            grad = in_ref[j, k] + in_ref[j, 2, 4 * k : 4 * k + 1] * grad


def scan_call(pieces):
    return pl.pallas_call(
        scan_kernel,
        out_shape=jax.ShapeDtypeStruct((16, 2, 8, LANES), F32),
        compiler_params=pltpu.CompilerParams(vmem_limit_bytes=SMALL_LIMIT),
    )(pieces)


def ring(a, b, n):
    return min((a - b) % n, (b - a) % n)


def hops(sender, receiver):
    def chip(ctx, smp):
        return smp // 4, (ctx % 2) * 2 + smp // 2 % 2, ctx // 2

    a, b = chip(*sender), chip(*receiver)
    return sum(ring(p, q, n) for p, q, n in zip(a, b, (4, 4, 8)))


def turned_places():
    pairs = []
    for s in range(16):
        way = [[hops((s, a), (k, s)) ** 3 for k in range(16)] for a in range(16)]
        pick = list(range(16))
        moved = True
        while moved:
            moved = False
            for a in range(16):
                for b in range(a):
                    if way[a][pick[b]] + way[b][pick[a]] < way[a][pick[a]] + way[b][pick[b]]:
                        pick[a], pick[b] = pick[b], pick[a]
                        moved = True
        pairs += [(s * 16 + a, pick[a] * 16 + s) for a in range(16)]
    return pairs


def swap(v, axis):
    return lax.all_to_all(v, axis, 0, 0, tiled=True)


def local(
    prompt_inputs,
    prompt_outgrad,
    prompt_bproj,
    prompt_cproj,
    prompt_decay,
    prompt_states,
    answer_inputs,
    answer_outgrad,
    answer_bproj,
    answer_cproj,
    answer_decay,
    answer_state,
):
    core = lax.axis_index("core").astype(jnp.int32)[None]
    side = lax.axis_index("yh").astype(jnp.int32)[None]
    other = [(0, 1), (1, 0)]
    a_x, a_dy, a_b, a_c = answer_inputs[0], answer_outgrad[0], answer_bproj[0], answer_cproj[0]

    a_rows, a_r, _, a_first = carry(a_dy, a_c, answer_decay[0], 2)
    a_turned = lax.ppermute(a_first, CTX + SMP, turned_places())
    p_rows, p_r, p_cum, p_first = carry(prompt_outgrad, prompt_cproj, prompt_decay, 3)
    a_keep, a_send = answer_call(a_x, a_dy, a_b, a_c, a_rows, a_r, answer_state, side, p_first)
    a_turned, a_keep, a_send = lax.optimization_barrier((a_turned, a_keep, a_send))
    a_got = lax.ppermute(a_send, "yh", other)
    shards = swap(jnp.concatenate([p_first, a_turned], axis=1), CTX)
    prompt_b, c_keep, c_send = prompt_call(
        prompt_inputs,
        prompt_outgrad,
        prompt_bproj,
        prompt_cproj,
        p_rows,
        p_r,
        prompt_states[0],
        core,
        a_keep,
    )
    grads, c_send, c_keep = lax.optimization_barrier((scan_call(shards), c_send, c_keep))
    entering = swap(grads, CTX)
    c_got = lax.ppermute(c_send, "core", other)
    answer_gx, c_sum = answer_x_call(a_dy, a_b, a_c, a_rows, a_r, c_keep, c_got, grads)
    a_got, answer_gx, c_sum = lax.optimization_barrier((a_got, answer_gx, c_sum))
    a_pair, entering = lax.optimization_barrier((a_keep + a_got, entering))
    answer_parts = swap(a_pair, "z")
    b_keep, b_send = finish_call(
        prompt_inputs, p_rows, p_cum, prompt_b, entering, core, answer_gx
    )
    b_got = lax.ppermute(b_send, "core", other)
    place = [lax.axis_index(name).astype(jnp.int32)[None] for name in ("x", "yl")]
    prompt_parts = shifted(merge_call(b_keep, b_got, c_sum, *place))
    prompt_gb, prompt_gc, answer_gb, answer_gc = sums_call(answer_parts, prompt_parts)
    prompt_gx = prompt_x_call(
        prompt_outgrad, prompt_bproj, prompt_cproj, p_rows, p_r, p_cum, entering, b_send
    )
    return prompt_gx, prompt_gb, prompt_gc, answer_gx[None], answer_gb[None], answer_gc[None]


def solution(mesh):
    split = Mesh(mesh.devices.reshape(8, 2, 4, 2, 2), CTX + SMP)
    in_specs = (
        P(CTX, SMP),
        P(CTX, SMP),
        P(CTX, None),
        P(CTX, None),
        P(SMP, CTX),
        P(CTX, SMP, None),
        P(SMP, None, CTX),
        P(SMP, None, CTX),
        P(SMP, None, None),
        P(SMP, None, None),
        P(SMP, CTX, None),
        P(CTX, None),
    )
    out_specs = (
        P(CTX, SMP),
        P(CTX + SMP, None),
        P(CTX + SMP, None),
        P(SMP, None, CTX),
        P(SMP, CTX, None),
        P(SMP, CTX, None),
    )
    return jax.shard_map(local, mesh=split, in_specs=in_specs, out_specs=out_specs, check_vma=False)
```

```python
import jax
import jax.numpy as jnp
from jax import lax
from jax.experimental import pallas as pl
from jax.experimental.pallas import tpu as pltpu
from jax.sharding import Mesh, PartitionSpec as P

CTX = ("z", "yh")
SMP = ("x", "yl", "core")
HEAD_DIM = 64
STATE = 128
BLOCK = 256
HEADS_DEV = 4
WIDTH = HEADS_DEV * HEAD_DIM
LANES = 128
F32 = jnp.float32
BF16 = jnp.bfloat16
LOG2E = 1.4426950408889634
VMEM_LIMIT = 60 * 1024 * 1024
SMALL_LIMIT = 24 * 1024 * 1024
STEP_BLOCKS = 4
CARRY_BLOCKS = 4


def iota(shape, dim):
    return lax.broadcasted_iota(jnp.int32, shape, dim)


def dot(a, b, dims=((1,), (0,))):
    return lax.dot_general(a, b, (dims, ((), ())), preferred_element_type=F32)


def split3(v):
    first = v.astype(BF16)
    rest = v - first.astype(F32)
    second = rest.astype(BF16)
    third = (rest - second.astype(F32)).astype(BF16)
    return first, second, third


def split2(v):
    first = v.astype(BF16)
    return first, (v - first.astype(F32)).astype(BF16)


def running_sums(logs):
    upper = (iota((BLOCK, BLOCK), 0) <= iota((BLOCK, BLOCK), 1)).astype(BF16)
    logs = logs * LOG2E
    parts = []
    for at in range(0, logs.shape[1], BLOCK):
        parts += [logs[:, at : at + BLOCK]] * 2
    one, two, three = split3(jnp.concatenate(parts, axis=0))
    return dot(one, upper) + dot(two, upper) + dot(three, upper)


def expand(rows, width):
    first = rows.astype(BF16).astype(F32)
    rest = rows - first
    second = rest.astype(BF16).astype(F32)
    parts = jnp.concatenate([first, second, rest - second, jnp.zeros_like(rows)], axis=0).astype(BF16)
    shape = (32, HEADS_DEV * width)
    lane = iota(shape, 1)
    pick = (iota(shape, 0) & 7) * width
    mine = ((lane >= pick) & (lane < pick + width)).astype(BF16)
    return dot(parts, mine, ((0,), (0,)))


def from_start(rows):
    return expand(jnp.exp2(rows), HEAD_DIM)


def to_end(rows):
    return expand(jnp.exp2(rows[:, BLOCK - 1 : BLOCK] - rows), HEAD_DIM)


def per_head(rows):
    spread = expand(rows, LANES)
    return [spread[:, h * LANES : (h + 1) * LANES] for h in range(HEADS_DEV)]


def spread_pieces(state, k):
    return state[:, k * LANES : (k + 1) * LANES].reshape(16, 8, LANES)


def carry_kernel(dy_ref, c_ref, logs_ref, rows_ref, r_ref, cum_ref, first_ref, r_scr, d_scr):
    step = pl.program_id(0)

    @pl.when(step == 0)
    def _():
        r_scr[...] = jnp.zeros_like(r_scr)
        d_scr[...] = jnp.ones_like(d_scr)
        rows_ref[...] = running_sums(logs_ref[...]).reshape(rows_ref.shape)

    last = pl.num_programs(0) - 1
    grad, dec = r_scr[...], d_scr[...]
    for j in range(CARRY_BLOCKS - 1, -1, -1):
        part = slice(j * BLOCK, (j + 1) * BLOCK)
        start = from_start(rows_ref[(last - step) * CARRY_BLOCKS + j])
        high, low = split2(dy_ref[part].astype(F32) * start)
        turned = c_ref[part].T
        final = start[BLOCK - 1 : BLOCK]
        r_ref[j] = grad
        cum_ref[j] = dec
        grad = final * grad + (dot(turned, high) + dot(turned, low))
        dec = final * dec
    r_scr[...], d_scr[...] = grad, dec

    @pl.when(step == last)
    def _():
        for k in range(2):
            first_ref[:, k] = spread_pieces(grad, k)
        if first_ref.shape[1] > 2:
            both = jnp.concatenate([dec[0:4, :LANES], dec[0:4, LANES:]], axis=0)
            first_ref[:, 2] = jnp.broadcast_to(both[None], (16, 8, LANES))


def cost(passes, moved):
    return pl.CostEstimate(flops=passes * 2 * BLOCK**3, bytes_accessed=moved, transcendentals=0)


def carry(dy, c, logs, tiles):
    blocks = dy.shape[0] // BLOCK
    steps = blocks // CARRY_BLOCKS
    span = CARRY_BLOCKS * BLOCK
    back = lambda i: (steps - 1 - i, 0)
    back3 = lambda i: (steps - 1 - i, 0, 0)
    return pl.pallas_call(
        carry_kernel,
        grid=(steps,),
        in_specs=[
            pl.BlockSpec((span, WIDTH), back),
            pl.BlockSpec((span, STATE), back),
            whole_spec(HEADS_DEV, blocks * BLOCK),
        ],
        out_specs=[
            whole_spec(blocks, 8, BLOCK),
            pl.BlockSpec((CARRY_BLOCKS, STATE, WIDTH), back3),
            pl.BlockSpec((CARRY_BLOCKS, 8, WIDTH), back3),
            whole_spec(16, tiles, 8, LANES),
        ],
        out_shape=[
            jax.ShapeDtypeStruct((blocks, 8, BLOCK), F32),
            jax.ShapeDtypeStruct((blocks, STATE, WIDTH), F32),
            jax.ShapeDtypeStruct((blocks, 8, WIDTH), F32),
            jax.ShapeDtypeStruct((16, tiles, 8, LANES), F32),
        ],
        scratch_shapes=[pltpu.VMEM((STATE, WIDTH), F32), pltpu.VMEM((8, WIDTH), F32)],
        compiler_params=pltpu.CompilerParams(vmem_limit_bytes=VMEM_LIMIT),
        cost_estimate=cost(32, 3 * 2**20),
    )(dy, c, logs)


def load_state(s0_ref, m_scr):
    for r in range(64):
        m_scr[4 * r : 4 * r + 4] = s0_ref[:, LANES * r : LANES * (r + 1)]
    low = iota((64, LANES), 1) < HEAD_DIM
    halves = []
    for k in range(2):
        one = m_scr[pl.ds(2 * k, 64, stride=4), :]
        two = m_scr[pl.ds(2 * k + 1, 64, stride=4), :]
        even = jnp.where(low, one, pltpu.roll(two, HEAD_DIM, 1))
        odd = jnp.where(low, pltpu.roll(one, HEAD_DIM, 1), two)
        halves.append(jnp.concatenate([even, odd], axis=0))
    parted = jnp.concatenate(halves, axis=1)
    row, col = iota((STATE, STATE), 0), iota((STATE, STATE), 1)
    order = (col == (row & 1) * 64 + (row >> 1)).astype(BF16)
    one, two, three = split3(parted)
    return dot(order, one) + dot(order, two) + dot(order, three)


def weights(rows, spread):
    half = BLOCK // 2
    keep = iota((half, half), 1) >= iota((half, half), 0)
    out = []
    for h in range(HEADS_DEV):
        row = rows[h : h + 1]
        top, bottom = spread[h][:half], spread[h][half:]
        left = jnp.where(keep, jnp.exp2(row[:, :half] - top), 0.0)
        right = jnp.exp2(row[:, half:] - top)
        w_bot = jnp.where(keep, jnp.exp2(row[:, half:] - bottom), 0.0)
        out.append((jnp.concatenate([left, right], axis=1), w_bot))
    return out


def proj_grads(x, dy, b, c, rows, r_in, state):
    half = BLOCK // 2
    cols = rows.T
    spread = [jnp.broadcast_to(cols[:, h : h + 1], (BLOCK, LANES)) for h in range(HEADS_DEV)]
    left = iota((BLOCK, LANES), 1) < HEAD_DIM
    run = jnp.concatenate(
        [jnp.where(left, spread[0], spread[1]), jnp.where(left, spread[2], spread[3])], axis=1
    )
    start = jnp.exp2(run)
    x_high, x_low = split2(x.astype(F32) * jnp.exp2(run[BLOCK - 1 : BLOCK] - run))
    dy_high, dy_low = split2(dy.astype(F32) * start)
    r_both = jnp.concatenate(split2(r_in), axis=0)
    s_both = jnp.concatenate(split2(state), axis=0)
    turned = b.T
    after = start[BLOCK - 1 : BLOCK] * state + (dot(turned, x_high) + dot(turned, x_low))

    lane_half = iota((BLOCK, LANES), 1)
    sum_top = jnp.zeros((half, BLOCK), F32)
    sum_bot = jnp.zeros((half, half), F32)
    for h, (w_top, w_bot) in enumerate(weights(rows, spread)):
        pair = slice((h // 2) * LANES, (h // 2 + 1) * LANES)
        mine = (lane_half < HEAD_DIM) if h % 2 == 0 else (lane_half >= HEAD_DIM)
        x_h = jnp.where(mine, x[:, pair], jnp.zeros((), BF16))
        dy_pair = dy[:, pair]
        sum_top = sum_top + w_top * dot(x_h[:half], dy_pair, ((1,), (1,)))
        sum_bot = sum_bot + w_bot * dot(x_h[half:], dy_pair[half:], ((1,), (1,)))
    w_top = sum_top.astype(BF16)
    w_bot = sum_bot.astype(BF16)
    b_state = dot(x_high, r_both, ((1,), (1,)))
    b_state = b_state[:, :STATE] + b_state[:, STATE:] + dot(x_low, r_both[:STATE], ((1,), (1,)))
    c_state = dot(dy_high, s_both, ((1,), (1,)))
    c_state = c_state[:, :STATE] + c_state[:, STATE:] + dot(dy_low, s_both[:STATE], ((1,), (1,)))
    b_top = b_state[:half] + dot(w_top, c)
    b_bot = b_state[half:] + dot(w_bot, c[half:])
    c_top = c_state[:half] + dot(w_top[:, :half], b[:half], ((0,), (0,)))
    c_bot = (
        c_state[half:]
        + dot(w_top[:, half:], b[:half], ((0,), (0,)))
        + dot(w_bot, b[half:], ((0,), (0,)))
    )
    return after, b_top, b_bot, c_top, c_bot


def input_grads(dy, b, c, rows, r_in):
    half = BLOCK // 2
    spread = per_head(rows)
    r_both = jnp.concatenate(split2(r_in), axis=0)
    bc_top = dot(b[:half], c, ((1,), (1,)))
    bc_bot = dot(b[half:], c[half:], ((1,), (1,)))
    lane = iota((BLOCK, WIDTH), 1)
    coeff_top, coeff_bot, dy_top, dy_bot = [], [], [], []
    for h, (w_top, w_bot) in enumerate(weights(rows, spread)):
        mine = (lane >= h * HEAD_DIM) & (lane < (h + 1) * HEAD_DIM)
        dy_h = jnp.where(mine, dy, jnp.zeros((), BF16))
        coeff_top.append((w_top * bc_top).astype(BF16))
        coeff_bot.append((w_bot * bc_bot).astype(BF16))
        dy_top.append(dy_h)
        dy_bot.append(dy_h[half:])
    from_r = to_end(rows) * dot(jnp.concatenate([b, b], axis=1), r_both)
    top = from_r[:half] + dot(jnp.concatenate(coeff_top, axis=1), jnp.concatenate(dy_top, axis=0))
    bottom = from_r[half:] + dot(jnp.concatenate(coeff_bot, axis=1), jnp.concatenate(dy_bot, axis=0))
    return top, bottom


def each_block(x_ref, dy_ref, b_ref, c_ref, rows_ref, r_ref, s0_ref, s_scr, m_scr):
    @pl.when(pl.program_id(0) == 0)
    def _():
        s_scr[...] = load_state(s0_ref, m_scr)

    state = s_scr[...]
    for j in range(STEP_BLOCKS):
        at = j * BLOCK
        part = slice(at, at + BLOCK)
        state, *grads = proj_grads(
            x_ref[part], dy_ref[part], b_ref[part], c_ref[part], rows_ref[j], r_ref[j], state
        )
        yield j, at, grads
    s_scr[...] = state


def answer_kernel(
    x_ref, dy_ref, b_ref, c_ref, rows_ref, r_ref, s0_ref, side_ref, after_ref, keep_ref, send_ref, s_scr, m_scr
):
    first = side_ref[0] == 0
    refs = (x_ref, dy_ref, b_ref, c_ref, rows_ref, r_ref, s0_ref, s_scr, m_scr)
    for j, _, (b_top, b_bot, c_top, c_bot) in each_block(*refs):
        keep_ref[j, 0:LANES] = jnp.where(first, b_top, b_bot)
        keep_ref[j, LANES:] = jnp.where(first, c_top, c_bot)
        send_ref[j, 0:LANES] = jnp.where(first, b_bot, b_top)
        send_ref[j, LANES:] = jnp.where(first, c_bot, c_top)


def prompt_kernel(
    x_ref, dy_ref, b_ref, c_ref, rows_ref, r_ref, s0_ref, core_ref, after_ref,
    b_out_ref, keep_ref, send_ref, s_scr, m_scr,
):
    first = core_ref[0] == 0
    refs = (x_ref, dy_ref, b_ref, c_ref, rows_ref, r_ref, s0_ref, s_scr, m_scr)
    for j, at, (b_top, b_bot, c_top, c_bot) in each_block(*refs):
        b_out_ref[at : at + LANES] = b_top
        b_out_ref[at + LANES : at + BLOCK] = b_bot
        keep_ref[j] = jnp.where(first, c_top, c_bot)
        send_ref[j] = jnp.where(first, c_bot, c_top)


def finish_kernel(
    x_ref, rows_ref, cum_ref, b_in_ref, enter_ref, core_ref, after_ref, keep_ref, send_ref, g_scr
):
    @pl.when(pl.program_id(0) == 0)
    def _():
        for k in range(2):
            high, low = split2(enter_ref[:, k].reshape(STATE, LANES))
            g_scr[:STATE, k * LANES : (k + 1) * LANES] = high
            g_scr[STATE:, k * LANES : (k + 1) * LANES] = low

    first = core_ref[0] == 0
    g_both = g_scr[...]
    for j in range(STEP_BLOCKS):
        part = slice(j * BLOCK, (j + 1) * BLOCK)
        scale = to_end(rows_ref[j]) * cum_ref[j, 0:1]
        high, low = split2(x_ref[part].astype(F32) * scale)
        fresh = dot(high, g_both, ((1,), (1,)))
        fresh = fresh[:, :STATE] + fresh[:, STATE:] + dot(low, g_both[:STATE], ((1,), (1,)))
        total = b_in_ref[part] + fresh
        keep_ref[j] = jnp.where(first, total[:LANES], total[LANES:])
        send_ref[j] = jnp.where(first, total[LANES:], total[:LANES])


def ways_kernel(*refs):
    ins, (x_ref, yl_ref), out_refs = refs[:-6], refs[-6:-4], refs[-4:]
    for dx, out_ref in enumerate(out_refs):
        for dy in range(2):
            to = ((x_ref[0] + dx) & 3) * 2 + (yl_ref[0] ^ dy)
            out_ref[dy] = ins[0][to] if len(ins) == 1 else ins[0][to] + ins[1][to]


def answer_x_kernel(
    dy_ref, b_ref, c_ref, rows_ref, r_ref, c_keep_ref, c_got_ref, after_ref, gx_ref, c_sum_ref
):
    c_sum_ref[...] = c_keep_ref[...] + c_got_ref[...]
    for j in range(STEP_BLOCKS):
        at = j * BLOCK
        part = slice(at, at + BLOCK)
        top, bottom = input_grads(dy_ref[part], b_ref[part], c_ref[part], rows_ref[j], r_ref[j])
        gx_ref[at : at + LANES] = top
        gx_ref[at + LANES : at + BLOCK] = bottom


def prompt_x_kernel(dy_ref, b_ref, c_ref, rows_ref, r_ref, cum_ref, enter_ref, after_ref, gx_ref, g_scr):
    @pl.when(pl.program_id(0) == 0)
    def _():
        for k in range(2):
            g_scr[:, k * LANES : (k + 1) * LANES] = enter_ref[:, k].reshape(STATE, LANES)

    for j in range(STEP_BLOCKS):
        at = j * BLOCK
        part = slice(at, at + BLOCK)
        r_in = r_ref[j] + cum_ref[j, 0:1] * g_scr[...]
        top, bottom = input_grads(dy_ref[part], b_ref[part], c_ref[part], rows_ref[j], r_in)
        gx_ref[at : at + LANES] = top
        gx_ref[at + LANES : at + BLOCK] = bottom


SPAN = STEP_BLOCKS * BLOCK


def tall_spec(width):
    return pl.BlockSpec((SPAN, width), lambda i: (i, 0))


def block_spec(*shape):
    return pl.BlockSpec((STEP_BLOCKS,) + shape, lambda i: (i,) + (0,) * len(shape))


def whole_spec(*shape):
    return pl.BlockSpec(shape, lambda i: (0,) * len(shape))


ROWS = block_spec(8, BLOCK)
STATES = block_spec(STATE, WIDTH)
DECAYS = block_spec(8, WIDTH)
ENTERING = whole_spec(16, 2, 8, LANES)
SCALAR = pl.BlockSpec(memory_space=pltpu.SMEM)
ORDER = pl.BlockSpec(memory_space=pl.ANY)


def call(kernel, in_specs, out_specs, out_shape, scratch, passes, args, limit=VMEM_LIMIT):
    return pl.pallas_call(
        kernel,
        grid=(args[0].shape[0] // SPAN,),
        in_specs=in_specs,
        out_specs=out_specs,
        out_shape=[jax.ShapeDtypeStruct(shape, F32) for shape in out_shape],
        scratch_shapes=[pltpu.VMEM(shape, kind) for shape, kind in scratch],
        compiler_params=pltpu.CompilerParams(vmem_limit_bytes=limit),
        cost_estimate=cost(passes, 6 * 2**20),
    )(*args)


MAIN = [tall_spec(WIDTH), tall_spec(WIDTH), tall_spec(STATE), tall_spec(STATE), ROWS, STATES]
MAIN += [whole_spec(HEADS_DEV, STATE * HEAD_DIM)]
MAIN_SCRATCH = [((STATE, WIDTH), F32), ((256, LANES), F32)]


def answer_call(*args):
    half = (args[0].shape[0] // BLOCK, BLOCK, LANES)
    specs = [block_spec(BLOCK, LANES)] * 2
    return call(answer_kernel, MAIN + [SCALAR, ORDER], specs, [half, half], MAIN_SCRATCH, 96, args)


def prompt_call(*args):
    length = args[0].shape[0]
    half = (length // BLOCK, LANES, LANES)
    specs = [tall_spec(STATE), block_spec(LANES, LANES), block_spec(LANES, LANES)]
    shapes = [(length, STATE), half, half]
    return call(prompt_kernel, MAIN + [SCALAR, ORDER], specs, shapes, MAIN_SCRATCH, 96, args)


def finish_call(*args):
    blocks = args[0].shape[0] // BLOCK
    half = block_spec(LANES, LANES)
    specs = [tall_spec(WIDTH), ROWS, DECAYS, tall_spec(STATE), ENTERING, SCALAR, ORDER]
    outs = [half, half]
    shapes = [(blocks, LANES, LANES), (blocks, LANES, LANES)]
    scratch = [((2 * STATE, WIDTH), BF16)]
    return call(finish_kernel, specs, outs, shapes, scratch, 32, args)


def ways(ins, place):
    vmem = pl.BlockSpec(memory_space=pltpu.VMEM)
    return pl.pallas_call(
        ways_kernel,
        in_specs=[vmem] * len(ins) + [SCALAR, SCALAR],
        out_specs=[vmem] * 4,
        out_shape=[jax.ShapeDtypeStruct((2, LANES, LANES), F32)] * 4,
        compiler_params=pltpu.CompilerParams(vmem_limit_bytes=SMALL_LIMIT),
    )(*ins, *place)


def along_x(parts):
    got = [parts[0]]
    for dx in (2, 1, 3):
        got.append(lax.ppermute(parts[dx], "x", [(x, (x + dx) % 4) for x in range(4)]))
    return got


def sum_x_kernel(*refs):
    ins, out_refs = refs[:8], refs[8:]
    for dy, out_ref in enumerate(out_refs):
        for k in range(2):
            one, two, three, four = (ref[dy] for ref in ins[4 * k : 4 * k + 4])
            out_ref[k * LANES : (k + 1) * LANES] = (one + two) + (three + four)


def sum_x(b_parts, c_parts):
    return pl.pallas_call(
        sum_x_kernel,
        out_shape=[jax.ShapeDtypeStruct((BLOCK, LANES), F32)] * 2,
        compiler_params=pltpu.CompilerParams(vmem_limit_bytes=SMALL_LIMIT),
    )(*b_parts, *c_parts)


def sums_kernel(z_ref, keep_ref, got_ref, pb_ref, pc_ref, ab_ref, ac_ref):
    prompt = keep_ref[...] + got_ref[...]
    answer = z_ref[0]
    for k in range(1, z_ref.shape[0]):
        answer = answer + z_ref[k]
    pb_ref[...] = prompt[:LANES]
    pc_ref[...] = prompt[LANES:]
    ab_ref[...] = answer[:LANES]
    ac_ref[...] = answer[LANES:]


def sums_call(answer_parts, keep, got):
    return pl.pallas_call(
        sums_kernel,
        out_shape=[jax.ShapeDtypeStruct((LANES, LANES), F32)] * 4,
        compiler_params=pltpu.CompilerParams(vmem_limit_bytes=SMALL_LIMIT),
    )(answer_parts, keep, got)


INPUT = [tall_spec(WIDTH), tall_spec(STATE), tall_spec(STATE), ROWS, STATES]


def answer_x_call(*args):
    half = block_spec(LANES, LANES)
    outs = [tall_spec(WIDTH), half]
    shapes = [args[0].shape, args[5].shape]
    return call(answer_x_kernel, INPUT + [half, half, ORDER], outs, shapes, [], 80, args)


def prompt_x_call(*args):
    out = [args[0].shape]
    specs = INPUT + [DECAYS, ENTERING, ORDER]
    scratch = [((STATE, WIDTH), F32)]
    return call(prompt_x_kernel, specs, [tall_spec(WIDTH)], out, scratch, 80, args)[0]


def scan_kernel(in_ref, out_ref):
    for k in range(2):
        grad = in_ref[0, 3 + k]
        for a in range(1, 16):
            grad = grad + in_ref[a, 3 + k]
        for j in range(15, -1, -1):
            out_ref[j, k] = grad
            grad = in_ref[j, k] + in_ref[j, 2, 4 * k : 4 * k + 1] * grad


def scan_call(pieces):
    return pl.pallas_call(
        scan_kernel,
        out_shape=jax.ShapeDtypeStruct((16, 2, 8, LANES), F32),
        compiler_params=pltpu.CompilerParams(vmem_limit_bytes=SMALL_LIMIT),
    )(pieces)


def ring(a, b, n):
    return min((a - b) % n, (b - a) % n)


def hops(sender, receiver):
    def chip(ctx, smp):
        return smp // 4, (ctx % 2) * 2 + smp // 2 % 2, ctx // 2

    a, b = chip(*sender), chip(*receiver)
    return sum(ring(p, q, n) for p, q, n in zip(a, b, (4, 4, 8)))


def turned_places():
    pairs = []
    for s in range(16):
        way = [[hops((s, a), (k, s)) ** 3 for k in range(16)] for a in range(16)]
        pick = list(range(16))
        moved = True
        while moved:
            moved = False
            for a in range(16):
                for b in range(a):
                    if way[a][pick[b]] + way[b][pick[a]] < way[a][pick[a]] + way[b][pick[b]]:
                        pick[a], pick[b] = pick[b], pick[a]
                        moved = True
        pairs += [(s * 16 + a, pick[a] * 16 + s) for a in range(16)]
    return pairs


def swap(v, axis):
    return lax.all_to_all(v, axis, 0, 0, tiled=True)


def local(
    prompt_inputs,
    prompt_outgrad,
    prompt_bproj,
    prompt_cproj,
    prompt_decay,
    prompt_states,
    answer_inputs,
    answer_outgrad,
    answer_bproj,
    answer_cproj,
    answer_decay,
    answer_state,
):
    core = lax.axis_index("core").astype(jnp.int32)[None]
    side = lax.axis_index("yh").astype(jnp.int32)[None]
    other = [(0, 1), (1, 0)]
    a_x, a_dy, a_b, a_c = answer_inputs[0], answer_outgrad[0], answer_bproj[0], answer_cproj[0]

    a_rows, a_r, _, a_first = carry(a_dy, a_c, answer_decay[0], 2)
    a_turned = lax.ppermute(a_first, CTX + SMP, turned_places())
    p_rows, p_r, p_cum, p_first = carry(prompt_outgrad, prompt_cproj, prompt_decay, 3)
    a_keep, a_send = answer_call(a_x, a_dy, a_b, a_c, a_rows, a_r, answer_state, side, p_first)
    a_turned, a_keep, a_send = lax.optimization_barrier((a_turned, a_keep, a_send))
    a_got = lax.ppermute(a_send, "yh", other)
    shards = swap(jnp.concatenate([p_first, a_turned], axis=1), CTX)
    prompt_b, c_keep, c_send = prompt_call(
        prompt_inputs,
        prompt_outgrad,
        prompt_bproj,
        prompt_cproj,
        p_rows,
        p_r,
        prompt_states[0],
        core,
        a_keep,
    )
    grads, c_send, c_keep = lax.optimization_barrier((scan_call(shards), c_send, c_keep))
    entering = swap(grads, CTX)
    c_got = lax.ppermute(c_send, "core", other)
    answer_gx, c_sum = answer_x_call(a_dy, a_b, a_c, a_rows, a_r, c_keep, c_got, grads)
    place = [lax.axis_index(name).astype(jnp.int32)[None] for name in ("x", "yl")]
    c_ways = ways((c_sum,), place)
    a_got, answer_gx, c_ways = lax.optimization_barrier((a_got, answer_gx, c_ways))
    c_parts = along_x(c_ways)
    a_pair, entering = lax.optimization_barrier((a_keep + a_got, entering))
    answer_parts = swap(a_pair, "z")
    b_keep, b_send = finish_call(
        prompt_inputs, p_rows, p_cum, prompt_b, entering, core, answer_gx
    )
    b_send, c_parts = lax.optimization_barrier((b_send, c_parts))
    b_got = lax.ppermute(b_send, "core", other)
    b_parts = along_x(ways((b_keep, b_got), place))
    prompt_gx = prompt_x_call(
        prompt_outgrad, prompt_bproj, prompt_cproj, p_rows, p_r, p_cum, entering, b_send
    )
    b_parts, prompt_gx = lax.optimization_barrier((b_parts, prompt_gx))
    p_keep, p_send = sum_x(b_parts, c_parts)
    p_got = lax.ppermute(p_send, "yl", other)
    prompt_gb, prompt_gc, answer_gb, answer_gc = sums_call(answer_parts, p_keep, p_got)
    return prompt_gx, prompt_gb, prompt_gc, answer_gx[None], answer_gb[None], answer_gc[None]


def solution(mesh):
    split = Mesh(mesh.devices.reshape(8, 2, 4, 2, 2), CTX + SMP)
    in_specs = (
        P(CTX, SMP),
        P(CTX, SMP),
        P(CTX, None),
        P(CTX, None),
        P(SMP, CTX),
        P(CTX, SMP, None),
        P(SMP, None, CTX),
        P(SMP, None, CTX),
        P(SMP, None, None),
        P(SMP, None, None),
        P(SMP, CTX, None),
        P(CTX, None),
    )
    out_specs = (
        P(CTX, SMP),
        P(CTX + SMP, None),
        P(CTX + SMP, None),
        P(SMP, None, CTX),
        P(SMP, CTX, None),
        P(SMP, CTX, None),
    )
    return jax.shard_map(local, mesh=split, in_specs=in_specs, out_specs=out_specs, check_vma=False)
```

```python
import jax
import jax.numpy as jnp
from jax import lax
from jax.experimental import pallas as pl
from jax.experimental.pallas import tpu as pltpu
from jax.sharding import Mesh, PartitionSpec as P

CTX = ("z", "yh")
SMP = ("x", "yl", "core")
HEAD_DIM = 64
STATE = 128
BLOCK = 256
HEADS_DEV = 4
WIDTH = HEADS_DEV * HEAD_DIM
LANES = 128
F32 = jnp.float32
BF16 = jnp.bfloat16
LOG2E = 1.4426950408889634
VMEM_LIMIT = 60 * 1024 * 1024
SMALL_LIMIT = 24 * 1024 * 1024
STEP_BLOCKS = 4
CARRY_BLOCKS = 8


def iota(shape, dim):
    return lax.broadcasted_iota(jnp.int32, shape, dim)


def dot(a, b, dims=((1,), (0,))):
    return lax.dot_general(a, b, (dims, ((), ())), preferred_element_type=F32)


def split3(v):
    first = v.astype(BF16)
    rest = v - first.astype(F32)
    second = rest.astype(BF16)
    third = (rest - second.astype(F32)).astype(BF16)
    return first, second, third


def split2(v):
    first = v.astype(BF16)
    return first, (v - first.astype(F32)).astype(BF16)


def running_sums(logs):
    upper = (iota((BLOCK, BLOCK), 0) <= iota((BLOCK, BLOCK), 1)).astype(BF16)
    logs = logs * LOG2E
    parts = []
    for at in range(0, logs.shape[1], BLOCK):
        parts += [logs[:, at : at + BLOCK]] * 2
    one, two, three = split3(jnp.concatenate(parts, axis=0))
    return dot(one, upper) + dot(two, upper) + dot(three, upper)


def expand(rows, width):
    first = rows.astype(BF16).astype(F32)
    rest = rows - first
    second = rest.astype(BF16).astype(F32)
    parts = jnp.concatenate([first, second, rest - second, jnp.zeros_like(rows)], axis=0).astype(BF16)
    shape = (32, HEADS_DEV * width)
    lane = iota(shape, 1)
    pick = (iota(shape, 0) & 7) * width
    mine = ((lane >= pick) & (lane < pick + width)).astype(BF16)
    return dot(parts, mine, ((0,), (0,)))


def from_start(rows):
    return expand(jnp.exp2(rows), HEAD_DIM)


def to_end(rows):
    return expand(jnp.exp2(rows[:, BLOCK - 1 : BLOCK] - rows), HEAD_DIM)


def per_head(rows):
    spread = expand(rows, LANES)
    return [spread[:, h * LANES : (h + 1) * LANES] for h in range(HEADS_DEV)]


def spread_pieces(state, k):
    return state[:, k * LANES : (k + 1) * LANES].reshape(16, 8, LANES)


def carry_kernel(dy_ref, c_ref, logs_ref, rows_ref, r_ref, cum_ref, first_ref, r_scr, d_scr):
    step = pl.program_id(0)

    @pl.when(step == 0)
    def _():
        r_scr[...] = jnp.zeros_like(r_scr)
        d_scr[...] = jnp.ones_like(d_scr)
        rows_ref[...] = running_sums(logs_ref[...]).reshape(rows_ref.shape)

    last = pl.num_programs(0) - 1
    grad, dec = r_scr[...], d_scr[...]
    for j in range(CARRY_BLOCKS - 1, -1, -1):
        part = slice(j * BLOCK, (j + 1) * BLOCK)
        start = from_start(rows_ref[(last - step) * CARRY_BLOCKS + j])
        high, low = split2(dy_ref[part].astype(F32) * start)
        turned = c_ref[part].T
        final = start[BLOCK - 1 : BLOCK]
        r_ref[j] = grad
        cum_ref[j] = dec
        grad = final * grad + (dot(turned, high) + dot(turned, low))
        dec = final * dec
    r_scr[...], d_scr[...] = grad, dec

    @pl.when(step == last)
    def _():
        for k in range(2):
            first_ref[:, k] = spread_pieces(grad, k)
        if first_ref.shape[1] > 2:
            both = jnp.concatenate([dec[0:4, :LANES], dec[0:4, LANES:]], axis=0)
            first_ref[:, 2] = jnp.broadcast_to(both[None], (16, 8, LANES))


def cost(passes, moved):
    return pl.CostEstimate(flops=passes * 2 * BLOCK**3, bytes_accessed=moved, transcendentals=0)


def carry(dy, c, logs, tiles):
    blocks = dy.shape[0] // BLOCK
    steps = blocks // CARRY_BLOCKS
    span = CARRY_BLOCKS * BLOCK
    back = lambda i: (steps - 1 - i, 0)
    back3 = lambda i: (steps - 1 - i, 0, 0)
    return pl.pallas_call(
        carry_kernel,
        grid=(steps,),
        in_specs=[
            pl.BlockSpec((span, WIDTH), back),
            pl.BlockSpec((span, STATE), back),
            whole_spec(HEADS_DEV, blocks * BLOCK),
        ],
        out_specs=[
            whole_spec(blocks, 8, BLOCK),
            pl.BlockSpec((CARRY_BLOCKS, STATE, WIDTH), back3),
            pl.BlockSpec((CARRY_BLOCKS, 8, WIDTH), back3),
            whole_spec(16, tiles, 8, LANES),
        ],
        out_shape=[
            jax.ShapeDtypeStruct((blocks, 8, BLOCK), F32),
            jax.ShapeDtypeStruct((blocks, STATE, WIDTH), F32),
            jax.ShapeDtypeStruct((blocks, 8, WIDTH), F32),
            jax.ShapeDtypeStruct((16, tiles, 8, LANES), F32),
        ],
        scratch_shapes=[pltpu.VMEM((STATE, WIDTH), F32), pltpu.VMEM((8, WIDTH), F32)],
        compiler_params=pltpu.CompilerParams(vmem_limit_bytes=VMEM_LIMIT),
        cost_estimate=cost(32, 3 * 2**20),
    )(dy, c, logs)


def load_state(s0_ref, m_scr):
    for r in range(64):
        m_scr[4 * r : 4 * r + 4] = s0_ref[:, LANES * r : LANES * (r + 1)]
    low = iota((64, LANES), 1) < HEAD_DIM
    halves = []
    for k in range(2):
        one = m_scr[pl.ds(2 * k, 64, stride=4), :]
        two = m_scr[pl.ds(2 * k + 1, 64, stride=4), :]
        even = jnp.where(low, one, pltpu.roll(two, HEAD_DIM, 1))
        odd = jnp.where(low, pltpu.roll(one, HEAD_DIM, 1), two)
        halves.append(jnp.concatenate([even, odd], axis=0))
    parted = jnp.concatenate(halves, axis=1)
    row, col = iota((STATE, STATE), 0), iota((STATE, STATE), 1)
    order = (col == (row & 1) * 64 + (row >> 1)).astype(BF16)
    one, two, three = split3(parted)
    return dot(order, one) + dot(order, two) + dot(order, three)


def weights(rows, spread):
    half = BLOCK // 2
    keep = iota((half, half), 1) >= iota((half, half), 0)
    out = []
    for h in range(HEADS_DEV):
        row = rows[h : h + 1]
        top, bottom = spread[h][:half], spread[h][half:]
        left = jnp.where(keep, jnp.exp2(row[:, :half] - top), 0.0)
        right = jnp.exp2(row[:, half:] - top)
        w_bot = jnp.where(keep, jnp.exp2(row[:, half:] - bottom), 0.0)
        out.append((jnp.concatenate([left, right], axis=1), w_bot))
    return out


def proj_grads(x, dy, b, c, rows, r_in, state):
    half = BLOCK // 2
    cols = rows.T
    spread = [jnp.broadcast_to(cols[:, h : h + 1], (BLOCK, LANES)) for h in range(HEADS_DEV)]
    left = iota((BLOCK, LANES), 1) < HEAD_DIM
    run = jnp.concatenate(
        [jnp.where(left, spread[0], spread[1]), jnp.where(left, spread[2], spread[3])], axis=1
    )
    start = jnp.exp2(run)
    x_high, x_low = split2(x.astype(F32) * jnp.exp2(run[BLOCK - 1 : BLOCK] - run))
    dy_high, dy_low = split2(dy.astype(F32) * start)
    r_both = jnp.concatenate(split2(r_in), axis=0)
    s_both = jnp.concatenate(split2(state), axis=0)
    turned = b.T
    after = start[BLOCK - 1 : BLOCK] * state + (dot(turned, x_high) + dot(turned, x_low))

    lane_half = iota((BLOCK, LANES), 1)
    sum_top = jnp.zeros((half, BLOCK), F32)
    sum_bot = jnp.zeros((half, half), F32)
    for h, (w_top, w_bot) in enumerate(weights(rows, spread)):
        pair = slice((h // 2) * LANES, (h // 2 + 1) * LANES)
        mine = (lane_half < HEAD_DIM) if h % 2 == 0 else (lane_half >= HEAD_DIM)
        x_h = jnp.where(mine, x[:, pair], jnp.zeros((), BF16))
        dy_pair = dy[:, pair]
        sum_top = sum_top + w_top * dot(x_h[:half], dy_pair, ((1,), (1,)))
        sum_bot = sum_bot + w_bot * dot(x_h[half:], dy_pair[half:], ((1,), (1,)))
    w_top = sum_top.astype(BF16)
    w_bot = sum_bot.astype(BF16)
    b_state = dot(x_high, r_both, ((1,), (1,)))
    b_state = b_state[:, :STATE] + b_state[:, STATE:] + dot(x_low, r_both[:STATE], ((1,), (1,)))
    c_state = dot(dy_high, s_both, ((1,), (1,)))
    c_state = c_state[:, :STATE] + c_state[:, STATE:] + dot(dy_low, s_both[:STATE], ((1,), (1,)))
    b_top = b_state[:half] + dot(w_top, c)
    b_bot = b_state[half:] + dot(w_bot, c[half:])
    c_top = c_state[:half] + dot(w_top[:, :half], b[:half], ((0,), (0,)))
    c_bot = (
        c_state[half:]
        + dot(w_top[:, half:], b[:half], ((0,), (0,)))
        + dot(w_bot, b[half:], ((0,), (0,)))
    )
    return after, b_top, b_bot, c_top, c_bot


def input_grads(dy, b, c, rows, r_in):
    half = BLOCK // 2
    spread = per_head(rows)
    r_both = jnp.concatenate(split2(r_in), axis=0)
    bc_top = dot(b[:half], c, ((1,), (1,)))
    bc_bot = dot(b[half:], c[half:], ((1,), (1,)))
    lane = iota((BLOCK, WIDTH), 1)
    coeff_top, coeff_bot, dy_top, dy_bot = [], [], [], []
    for h, (w_top, w_bot) in enumerate(weights(rows, spread)):
        mine = (lane >= h * HEAD_DIM) & (lane < (h + 1) * HEAD_DIM)
        dy_h = jnp.where(mine, dy, jnp.zeros((), BF16))
        coeff_top.append((w_top * bc_top).astype(BF16))
        coeff_bot.append((w_bot * bc_bot).astype(BF16))
        dy_top.append(dy_h)
        dy_bot.append(dy_h[half:])
    from_r = to_end(rows) * dot(jnp.concatenate([b, b], axis=1), r_both)
    top = from_r[:half] + dot(jnp.concatenate(coeff_top, axis=1), jnp.concatenate(dy_top, axis=0))
    bottom = from_r[half:] + dot(jnp.concatenate(coeff_bot, axis=1), jnp.concatenate(dy_bot, axis=0))
    return top, bottom


def each_block(x_ref, dy_ref, b_ref, c_ref, rows_ref, r_ref, s0_ref, s_scr, m_scr):
    @pl.when(pl.program_id(0) == 0)
    def _():
        s_scr[...] = load_state(s0_ref, m_scr)

    state = s_scr[...]
    for j in range(STEP_BLOCKS):
        at = j * BLOCK
        part = slice(at, at + BLOCK)
        state, *grads = proj_grads(
            x_ref[part], dy_ref[part], b_ref[part], c_ref[part], rows_ref[j], r_ref[j], state
        )
        yield j, at, grads
    s_scr[...] = state


def answer_kernel(
    x_ref, dy_ref, b_ref, c_ref, rows_ref, r_ref, s0_ref, side_ref, after_ref, keep_ref, send_ref, s_scr, m_scr
):
    first = side_ref[0] == 0
    refs = (x_ref, dy_ref, b_ref, c_ref, rows_ref, r_ref, s0_ref, s_scr, m_scr)
    for j, _, (b_top, b_bot, c_top, c_bot) in each_block(*refs):
        keep_ref[j, 0:LANES] = jnp.where(first, b_top, b_bot)
        keep_ref[j, LANES:] = jnp.where(first, c_top, c_bot)
        send_ref[j, 0:LANES] = jnp.where(first, b_bot, b_top)
        send_ref[j, LANES:] = jnp.where(first, c_bot, c_top)


def prompt_kernel(
    x_ref, dy_ref, b_ref, c_ref, rows_ref, r_ref, s0_ref, core_ref, after_ref,
    b_out_ref, keep_ref, send_ref, s_scr, m_scr,
):
    first = core_ref[0] == 0
    refs = (x_ref, dy_ref, b_ref, c_ref, rows_ref, r_ref, s0_ref, s_scr, m_scr)
    for j, at, (b_top, b_bot, c_top, c_bot) in each_block(*refs):
        b_out_ref[at : at + LANES] = b_top
        b_out_ref[at + LANES : at + BLOCK] = b_bot
        keep_ref[j] = jnp.where(first, c_top, c_bot)
        send_ref[j] = jnp.where(first, c_bot, c_top)


def finish_kernel(
    x_ref, rows_ref, cum_ref, b_in_ref, enter_ref, core_ref, after_ref, keep_ref, send_ref, g_scr
):
    @pl.when(pl.program_id(0) == 0)
    def _():
        for k in range(2):
            high, low = split2(enter_ref[:, k].reshape(STATE, LANES))
            g_scr[:STATE, k * LANES : (k + 1) * LANES] = high
            g_scr[STATE:, k * LANES : (k + 1) * LANES] = low

    first = core_ref[0] == 0
    g_both = g_scr[...]
    for j in range(STEP_BLOCKS):
        part = slice(j * BLOCK, (j + 1) * BLOCK)
        scale = to_end(rows_ref[j]) * cum_ref[j, 0:1]
        high, low = split2(x_ref[part].astype(F32) * scale)
        fresh = dot(high, g_both, ((1,), (1,)))
        fresh = fresh[:, :STATE] + fresh[:, STATE:] + dot(low, g_both[:STATE], ((1,), (1,)))
        total = b_in_ref[part] + fresh
        keep_ref[j] = jnp.where(first, total[:LANES], total[LANES:])
        send_ref[j] = jnp.where(first, total[LANES:], total[:LANES])


def ways_kernel(*refs):
    ins, (x_ref, yl_ref), out_refs = refs[:-6], refs[-6:-4], refs[-4:]
    for dx, out_ref in enumerate(out_refs):
        for dy in range(2):
            to = ((x_ref[0] + dx) & 3) * 2 + (yl_ref[0] ^ dy)
            out_ref[dy] = ins[0][to] if len(ins) == 1 else ins[0][to] + ins[1][to]


def answer_x_kernel(
    dy_ref, b_ref, c_ref, rows_ref, r_ref, c_keep_ref, c_got_ref, after_ref, gx_ref, c_sum_ref
):
    c_sum_ref[...] = c_keep_ref[...] + c_got_ref[...]
    for j in range(STEP_BLOCKS):
        at = j * BLOCK
        part = slice(at, at + BLOCK)
        top, bottom = input_grads(dy_ref[part], b_ref[part], c_ref[part], rows_ref[j], r_ref[j])
        gx_ref[at : at + LANES] = top
        gx_ref[at + LANES : at + BLOCK] = bottom


def prompt_x_kernel(dy_ref, b_ref, c_ref, rows_ref, r_ref, cum_ref, enter_ref, after_ref, *refs):
    gx_ref, g_scr = refs[-2:]
    @pl.when(pl.program_id(0) == 0)
    def _():
        for k in range(2):
            g_scr[:, k * LANES : (k + 1) * LANES] = enter_ref[:, k].reshape(STATE, LANES)

    for j in range(STEP_BLOCKS):
        at = j * BLOCK
        part = slice(at, at + BLOCK)
        r_in = r_ref[j] + cum_ref[j, 0:1] * g_scr[...]
        top, bottom = input_grads(dy_ref[part], b_ref[part], c_ref[part], rows_ref[j], r_in)
        gx_ref[at : at + LANES] = top
        gx_ref[at + LANES : at + BLOCK] = bottom


SPAN = STEP_BLOCKS * BLOCK


def tall_spec(width):
    return pl.BlockSpec((SPAN, width), lambda i: (i, 0))


def block_spec(*shape):
    return pl.BlockSpec((STEP_BLOCKS,) + shape, lambda i: (i,) + (0,) * len(shape))


def whole_spec(*shape):
    return pl.BlockSpec(shape, lambda i: (0,) * len(shape))


ROWS = block_spec(8, BLOCK)
STATES = block_spec(STATE, WIDTH)
DECAYS = block_spec(8, WIDTH)
ENTERING = whole_spec(16, 2, 8, LANES)
SCALAR = pl.BlockSpec(memory_space=pltpu.SMEM)
ORDER = pl.BlockSpec(memory_space=pl.ANY)


def call(kernel, in_specs, out_specs, out_shape, scratch, passes, args, limit=VMEM_LIMIT):
    return pl.pallas_call(
        kernel,
        grid=(args[0].shape[0] // SPAN,),
        in_specs=in_specs,
        out_specs=out_specs,
        out_shape=[jax.ShapeDtypeStruct(shape, F32) for shape in out_shape],
        scratch_shapes=[pltpu.VMEM(shape, kind) for shape, kind in scratch],
        compiler_params=pltpu.CompilerParams(vmem_limit_bytes=limit),
        cost_estimate=cost(passes, 6 * 2**20),
    )(*args)


MAIN = [tall_spec(WIDTH), tall_spec(WIDTH), tall_spec(STATE), tall_spec(STATE), ROWS, STATES]
MAIN += [whole_spec(HEADS_DEV, STATE * HEAD_DIM)]
MAIN_SCRATCH = [((STATE, WIDTH), F32), ((256, LANES), F32)]


def answer_call(*args):
    half = (args[0].shape[0] // BLOCK, BLOCK, LANES)
    specs = [block_spec(BLOCK, LANES)] * 2
    return call(answer_kernel, MAIN + [SCALAR, ORDER], specs, [half, half], MAIN_SCRATCH, 96, args)


def prompt_call(*args):
    length = args[0].shape[0]
    half = (length // BLOCK, LANES, LANES)
    specs = [tall_spec(STATE), block_spec(LANES, LANES), block_spec(LANES, LANES)]
    shapes = [(length, STATE), half, half]
    return call(prompt_kernel, MAIN + [SCALAR, ORDER], specs, shapes, MAIN_SCRATCH, 96, args)


def finish_call(*args):
    blocks = args[0].shape[0] // BLOCK
    half = block_spec(LANES, LANES)
    specs = [tall_spec(WIDTH), ROWS, DECAYS, tall_spec(STATE), ENTERING, SCALAR, ORDER]
    outs = [half, half]
    shapes = [(blocks, LANES, LANES), (blocks, LANES, LANES)]
    scratch = [((2 * STATE, WIDTH), BF16)]
    return call(finish_kernel, specs, outs, shapes, scratch, 32, args)


def ways(ins, place):
    vmem = pl.BlockSpec(memory_space=pltpu.VMEM)
    return pl.pallas_call(
        ways_kernel,
        in_specs=[vmem] * len(ins) + [SCALAR, SCALAR],
        out_specs=[vmem] * 4,
        out_shape=[jax.ShapeDtypeStruct((2, LANES, LANES), F32)] * 4,
        compiler_params=pltpu.CompilerParams(vmem_limit_bytes=SMALL_LIMIT),
    )(*ins, *place)


def along_x(parts):
    got = [parts[0]]
    for dx in (2, 1, 3):
        got.append(lax.ppermute(parts[dx], "x", [(x, (x + dx) % 4) for x in range(4)]))
    return got


def sum_x_kernel(*refs):
    ins, out_refs = refs[:8], refs[8:]
    for dy, out_ref in enumerate(out_refs):
        for k in range(2):
            one, two, three, four = (ref[dy] for ref in ins[4 * k : 4 * k + 4])
            out_ref[k * LANES : (k + 1) * LANES] = (one + two) + (three + four)


def sum_x(b_parts, c_parts):
    return pl.pallas_call(
        sum_x_kernel,
        out_shape=[jax.ShapeDtypeStruct((BLOCK, LANES), F32)] * 2,
        compiler_params=pltpu.CompilerParams(vmem_limit_bytes=SMALL_LIMIT),
    )(*b_parts, *c_parts)


def sums_kernel(z_ref, keep_ref, got_ref, pb_ref, pc_ref, ab_ref, ac_ref):
    prompt = keep_ref[...] + got_ref[...]
    answer = z_ref[0]
    for k in range(1, z_ref.shape[0]):
        answer = answer + z_ref[k]
    pb_ref[...] = prompt[:LANES]
    pc_ref[...] = prompt[LANES:]
    ab_ref[...] = answer[:LANES]
    ac_ref[...] = answer[LANES:]


def sums_call(answer_parts, keep, got):
    return pl.pallas_call(
        sums_kernel,
        out_shape=[jax.ShapeDtypeStruct((LANES, LANES), F32)] * 4,
        compiler_params=pltpu.CompilerParams(vmem_limit_bytes=SMALL_LIMIT),
    )(answer_parts, keep, got)


INPUT = [tall_spec(WIDTH), tall_spec(STATE), tall_spec(STATE), ROWS, STATES]


def answer_x_call(*args):
    half = block_spec(LANES, LANES)
    outs = [tall_spec(WIDTH), half]
    shapes = [args[0].shape, args[5].shape]
    return call(answer_x_kernel, INPUT + [half, half, ORDER], outs, shapes, [], 80, args)


def prompt_x_part(args, part, into=()):
    at = lambda *shape: pl.BlockSpec(shape, lambda i: (i + part,) + (0,) * (len(shape) - 1))
    wide, thin = at(SPAN, WIDTH), at(SPAN, STATE)
    specs = [wide, thin, thin, at(STEP_BLOCKS, 8, BLOCK), at(STEP_BLOCKS, STATE, WIDTH)]
    specs += [at(STEP_BLOCKS, 8, WIDTH), ENTERING, ORDER]
    return pl.pallas_call(
        prompt_x_kernel,
        grid=(1,),
        in_specs=specs + [ORDER] * len(into),
        out_specs=wide,
        out_shape=jax.ShapeDtypeStruct(args[0].shape, F32),
        input_output_aliases={len(specs): 0} if into else {},
        scratch_shapes=[pltpu.VMEM((STATE, WIDTH), F32)],
        compiler_params=pltpu.CompilerParams(vmem_limit_bytes=VMEM_LIMIT),
        cost_estimate=cost(40, 3 * 2**20),
    )(*args, *into)


def scan_kernel(in_ref, out_ref):
    for k in range(2):
        grad = in_ref[0, 3 + k]
        for a in range(1, 16):
            grad = grad + in_ref[a, 3 + k]
        for j in range(15, -1, -1):
            out_ref[j, k] = grad
            grad = in_ref[j, k] + in_ref[j, 2, 4 * k : 4 * k + 1] * grad


def scan_call(pieces):
    return pl.pallas_call(
        scan_kernel,
        out_shape=jax.ShapeDtypeStruct((16, 2, 8, LANES), F32),
        compiler_params=pltpu.CompilerParams(vmem_limit_bytes=SMALL_LIMIT),
    )(pieces)


def ring(a, b, n):
    return min((a - b) % n, (b - a) % n)


def hops(sender, receiver):
    def chip(ctx, smp):
        return smp // 4, (ctx % 2) * 2 + smp // 2 % 2, ctx // 2

    a, b = chip(*sender), chip(*receiver)
    return sum(ring(p, q, n) for p, q, n in zip(a, b, (4, 4, 8)))


def turned_places():
    pairs = []
    for s in range(16):
        way = [[hops((s, a), (k, s)) ** 3 for k in range(16)] for a in range(16)]
        pick = list(range(16))
        moved = True
        while moved:
            moved = False
            for a in range(16):
                for b in range(a):
                    if way[a][pick[b]] + way[b][pick[a]] < way[a][pick[a]] + way[b][pick[b]]:
                        pick[a], pick[b] = pick[b], pick[a]
                        moved = True
        pairs += [(s * 16 + a, pick[a] * 16 + s) for a in range(16)]
    return pairs


def swap(v, axis):
    return lax.all_to_all(v, axis, 0, 0, tiled=True)


def local(
    prompt_inputs,
    prompt_outgrad,
    prompt_bproj,
    prompt_cproj,
    prompt_decay,
    prompt_states,
    answer_inputs,
    answer_outgrad,
    answer_bproj,
    answer_cproj,
    answer_decay,
    answer_state,
):
    core = lax.axis_index("core").astype(jnp.int32)[None]
    side = lax.axis_index("yh").astype(jnp.int32)[None]
    other = [(0, 1), (1, 0)]
    a_x, a_dy, a_b, a_c = answer_inputs[0], answer_outgrad[0], answer_bproj[0], answer_cproj[0]

    a_rows, a_r, _, a_first = carry(a_dy, a_c, answer_decay[0], 2)
    a_turned = lax.ppermute(a_first, CTX + SMP, turned_places())
    p_rows, p_r, p_cum, p_first = carry(prompt_outgrad, prompt_cproj, prompt_decay, 3)
    a_keep, a_send = answer_call(a_x, a_dy, a_b, a_c, a_rows, a_r, answer_state, side, p_first)
    a_turned, a_keep, a_send = lax.optimization_barrier((a_turned, a_keep, a_send))
    a_got = lax.ppermute(a_send, "yh", other)
    shards = swap(jnp.concatenate([p_first, a_turned], axis=1), CTX)
    prompt_b, c_keep, c_send = prompt_call(
        prompt_inputs,
        prompt_outgrad,
        prompt_bproj,
        prompt_cproj,
        p_rows,
        p_r,
        prompt_states[0],
        core,
        a_keep,
    )
    grads, c_send, c_keep = lax.optimization_barrier((scan_call(shards), c_send, c_keep))
    entering = swap(grads, CTX)
    c_got = lax.ppermute(c_send, "core", other)
    answer_gx, c_sum = answer_x_call(a_dy, a_b, a_c, a_rows, a_r, c_keep, c_got, grads)
    place = [lax.axis_index(name).astype(jnp.int32)[None] for name in ("x", "yl")]
    c_ways = ways((c_sum,), place)
    a_got, answer_gx, c_ways = lax.optimization_barrier((a_got, answer_gx, c_ways))
    c_parts = along_x(c_ways)
    a_pair, entering = lax.optimization_barrier((a_keep + a_got, entering))
    answer_parts = swap(a_pair, "z")
    b_keep, b_send = finish_call(
        prompt_inputs, p_rows, p_cum, prompt_b, entering, core, answer_gx
    )
    b_send, c_parts = lax.optimization_barrier((b_send, c_parts))
    b_got = lax.ppermute(b_send, "core", other)
    b_parts = along_x(ways((b_keep, b_got), place))
    last = (prompt_outgrad, prompt_bproj, prompt_cproj, p_rows, p_r, p_cum, entering)
    prompt_gx = prompt_x_part(last + (b_send,), 0)
    b_parts, prompt_gx = lax.optimization_barrier((b_parts, prompt_gx))
    p_keep, p_send = sum_x(b_parts, c_parts)
    p_got = lax.ppermute(p_send, "yl", other)
    prompt_gx = prompt_x_part(last + (p_send,), 1, (prompt_gx,))
    prompt_gb, prompt_gc, answer_gb, answer_gc = sums_call(answer_parts, p_keep, p_got)
    return prompt_gx, prompt_gb, prompt_gc, answer_gx[None], answer_gb[None], answer_gc[None]


def solution(mesh):
    split = Mesh(mesh.devices.reshape(8, 2, 4, 2, 2), CTX + SMP)
    in_specs = (
        P(CTX, SMP),
        P(CTX, SMP),
        P(CTX, None),
        P(CTX, None),
        P(SMP, CTX),
        P(CTX, SMP, None),
        P(SMP, None, CTX),
        P(SMP, None, CTX),
        P(SMP, None, None),
        P(SMP, None, None),
        P(SMP, CTX, None),
        P(CTX, None),
    )
    out_specs = (
        P(CTX, SMP),
        P(CTX + SMP, None),
        P(CTX + SMP, None),
        P(SMP, None, CTX),
        P(SMP, CTX, None),
        P(SMP, CTX, None),
    )
    return jax.shard_map(local, mesh=split, in_specs=in_specs, out_specs=out_specs, check_vma=False)
```
